256 devices in a mesh: polar: 32 (over z, y), azimuth: 8 (over x, core).
Axes of the slice: x: 4, y: 4, z: 8, core: 2. Of those that a mesh axis runs over, the one named last changes fastest.
Arguments:
- field: bfloat16 [768, 1440, 256], P('polar', 'azimuth'), may hold values from -6 to 6
- cotangent: bfloat16 [768, 1440, 256], P('polar', 'azimuth'), may hold values from -6 to 6
- legendre: bfloat16 [512, 768, 512], P(('polar', 'azimuth')), may hold values from -0.0625 to 0.0625, as said below
- lat_weight: float32 [768], replicated, may hold values from 0.5 to 2
- filter_weight: bfloat16 [512, 256, 256], P('polar'), may hold values from -0.375 to 0.375
- wave_order: int32 [512], replicated, may hold values from 0 to 511, as said below
- deg_order: int32 [64], replicated, may hold values from 0 to 63, as said below
Outputs:
- output: bfloat16 [768, 1440, 256], P('polar', 'azimuth')
- grad_field: bfloat16 [768, 1440, 256], P('polar', 'azimuth')
- grad_weight: float32 [512, 256, 256], P('polar', 'azimuth')
The draws below stay inside these ranges and needn't reach their ends.
Inputs may be any that keep to these rules, and one draw needn't show every extreme that they name: `wave_order`: a permutation of the 512 wavenumbers; the 2 slots of one device (devices in polar+azimuth order) hold pairs m and 511 - m. `deg_order`: a permutation of the 64 degree blocks; the 2 block slots of one polar index hold pairs b and 63 - b. legendre[k, a, l] is 0 where l < wave_order[k].
All inputs are finite; a program needn't handle non-finite values.
Results may differ from the reference program's by a relative error of at most 0.023.
Values may be sent and summed in bfloat16 or wider, within the bound.
No kernel may reach another device: no remote copies, remote signals or barrier semaphores. Data moves between devices by JAX's collectives and lax.ppermute only.
A program may use at most 192 MiB of HBM per device.

```python
import math
import jax
import jax.numpy as jnp
from jax import lax

C = 256
NLON = 1440
L = 512
NBLK = 64
M = 512
NLAT = 768
DB = 8


def folded_pairs(key, entry_count):
    half_count = entry_count // 2
    chosen = jax.random.permutation(key, half_count).astype(jnp.int32)
    return jnp.stack([chosen, entry_count - 1 - chosen], axis=1).reshape(entry_count)


def wave_slots(key):
    return folded_pairs(jax.random.fold_in(key, 11), M)


def draw_wave_order(key, part):
    return wave_slots(key)


def draw_deg_order(key, part):
    key = jax.random.fold_in(key, 7)
    return folded_pairs(key, NBLK)


def draw_legendre(key, part):
    slot_order = wave_slots(key)
    key = jax.random.fold_in(key, 5)
    values = jax.random.uniform(key, (M, NLAT, L), jnp.float32, -0.0625, 0.0625)
    degree = jnp.arange(L, dtype=jnp.int32)
    upper_part = degree[None, None, :] >= slot_order[:, None, None]
    return jnp.where(upper_part, values, 0.0).astype(jnp.bfloat16)


def steps_of(rng, dims, shards, least, largest):
    factor_of, own = 1.0, jax.random.fold_in(rng, 6)
    for axis_at, parts in shards:
        heights = jnp.exp(jax.random.uniform(jax.random.fold_in(own, axis_at), (parts,), jnp.float32, least / len(shards), largest / len(shards)))
        factor_of = factor_of * jnp.repeat(heights, dims[axis_at] // parts).reshape([-1 if axis == axis_at else 1 for axis in range(len(dims))])
    return factor_of


def gaussian(own_key, dims, width, bound, cuts=(), held_as=jnp.bfloat16):
    entries = width * jax.random.normal(own_key, dims, jnp.float32)
    if cuts:
        entries = entries * steps_of(own_key, dims, cuts, -0.22, 0.18)
    return jnp.clip(entries, -bound, bound).astype(held_as)


def setup_inputs(seed: int = 0) -> dict:
    keys = jax.random.split(jax.random.key(seed), 8)
    return {
        "field": gaussian(keys[0], (NLAT, NLON, C), 1.0, 6.0, ((0, 32), (1, 8))),
        "cotangent": gaussian(keys[1], (NLAT, NLON, C), 1.0, 6.0, ((0, 32), (1, 8))),
        "legendre": draw_legendre(jax.random.fold_in(keys[7], 71), 0),
        "lat_weight": jnp.clip(jnp.exp(jax.random.uniform(keys[3], (NLAT,), jnp.float32, math.log(0.5), math.log(2.0))), 0.5, 2.0),
        "filter_weight": gaussian(keys[4], (L, C, C), C ** -0.5, 0.375, ((0, 32),)),
        "wave_order": draw_wave_order(jax.random.fold_in(keys[7], 71), 0),
        "deg_order": draw_deg_order(jax.random.fold_in(keys[7], 71), 0),
    }


def twiddle(slot_order, lon_count, doubled):
    longitude = jnp.arange(lon_count, dtype=jnp.int32)
    turns = longitude[:, None] * slot_order[None, :] % lon_count
    angle = 2.0 * math.pi / lon_count * turns.astype(jnp.float32)
    factor = jnp.full(slot_order.shape, 1.0 / math.sqrt(lon_count), jnp.float32)
    if doubled:
        factor = factor * jnp.where(slot_order == 0, 1.0, 2.0).astype(jnp.float32)
    stacked = jnp.stack([jnp.cos(angle), -jnp.sin(angle)], axis=1) * factor[None, None, :]
    return stacked.astype(jnp.bfloat16)

def analysis_step(operands):
    table_plane, column_data = operands
    return jnp.dot(table_plane.T, column_data, preferred_element_type=jnp.float32).astype(jnp.bfloat16)

def synthesis_step(operands):
    table_plane, column_data = operands
    return jnp.dot(table_plane, column_data, preferred_element_type=jnp.float32)

def reference(field, cotangent, legendre, lat_weight, filter_weight, wave_order, deg_order):
    plain_table = twiddle(wave_order, NLON, False).astype(jnp.float32)
    doubled_table = twiddle(wave_order, NLON, True).astype(jnp.float32)
    field_wide = field.astype(jnp.float32)
    spectrum = jnp.einsum('anc,nrk->karc', field_wide, plain_table).astype(jnp.bfloat16)
    spectrum = spectrum.reshape(M, NLAT, 2 * C)
    weighted = (spectrum.astype(jnp.float32) * lat_weight[None, :, None]).astype(jnp.bfloat16)
    coeffs = lax.map(analysis_step, (legendre, weighted))
    natural_weight = filter_weight.reshape(NBLK, DB, C, C)[jnp.argsort(deg_order)]
    natural_weight = natural_weight.reshape(L, C, C).astype(jnp.float32)

    def apply_filter(coefficient):
        shaped = coefficient.reshape(L, 2, C).astype(jnp.float32)
        return jnp.einsum('lrc,lce->lre', shaped, natural_weight).astype(jnp.bfloat16).reshape(L, 2 * C)

    def reverse_filter(coefficient):
        shaped = coefficient.reshape(L, 2, C).astype(jnp.float32)
        return jnp.einsum('lre,lce->lrc', shaped, natural_weight).astype(jnp.bfloat16).reshape(L, 2 * C)
    filtered = lax.map(apply_filter, coeffs)
    grid_spec = lax.map(synthesis_step, (legendre, filtered)).astype(jnp.bfloat16)
    linear = jnp.einsum('karc,nrk->anc', grid_spec.reshape(M, NLAT, 2, C).astype(jnp.float32), doubled_table)
    linear = linear.astype(jnp.bfloat16)
    activated, pullback = jax.vjp(jax.nn.gelu, linear.astype(jnp.float32))
    output = (field_wide + activated).astype(jnp.bfloat16)
    cotangent_wide = cotangent.astype(jnp.float32)
    grad_linear = pullback(cotangent_wide)[0].astype(jnp.bfloat16)
    grad_spec = jnp.einsum('anc,nrk->karc', grad_linear.astype(jnp.float32), doubled_table).astype(jnp.bfloat16)
    grad_spec = grad_spec.reshape(M, NLAT, 2 * C)
    grad_filtered = lax.map(analysis_step, (legendre, grad_spec))
    natural_grad = jnp.einsum('klrc,klre->lce', coeffs.reshape(M, L, 2, C).astype(jnp.float32), grad_filtered.reshape(M, L, 2, C).astype(jnp.float32))
    grad_weight = natural_grad.reshape(NBLK, DB, C, C)[deg_order].reshape(L, C, C)
    grad_coeffs = lax.map(reverse_filter, grad_filtered)
    grad_weighted = lax.map(synthesis_step, (legendre, grad_coeffs)) * lat_weight[None, :, None]
    grad_weighted = grad_weighted.astype(jnp.bfloat16)
    grad_grid = jnp.einsum('karc,nrk->anc', grad_weighted.reshape(M, NLAT, 2, C).astype(jnp.float32), plain_table)
    grad_grid = grad_grid.astype(jnp.bfloat16)
    grad_field = (cotangent_wide + grad_grid.astype(jnp.float32)).astype(jnp.bfloat16)
    return (output, grad_field, grad_weight)
```

```python
import functools
import math

import jax
import jax.numpy as jnp
from jax import lax
from jax.experimental import pallas as pl
from jax.experimental.pallas import tpu as pltpu
from jax.sharding import PartitionSpec as P

BF16 = jnp.bfloat16
F32 = jnp.float32
LANES = 128
ROW_PAD = 192
MIB = 1024 * 1024
GELU_A = math.sqrt(2.0 / math.pi)
GELU_B = 0.044715


def exchange(payload, axes):
    return lax.all_to_all(payload, axes, split_axis=0, concat_axis=0, tiled=True)


def call(kernel, out_shape, scratch, vmem_mib, flops, moved, *operands):
    whole = pl.BlockSpec(memory_space=pltpu.VMEM)
    outs = jax.tree.map(lambda _: whole, out_shape)
    return pl.pallas_call(
        kernel,
        out_shape=out_shape,
        in_specs=[whole] * len(operands),
        out_specs=outs,
        scratch_shapes=scratch,
        compiler_params=pltpu.CompilerParams(vmem_limit_bytes=vmem_mib * MIB),
        cost_estimate=pl.CostEstimate(flops=flops, bytes_accessed=moved, transcendentals=0),
    )(*operands)


def message_row(row, half, slot, part):
    return row * 8 + half * 4 + slot * 2 + part


def unpack_rows(received, wide, row, slot, part, peers):
    halves = [
        wide[pl.ds(message_row(row, half, slot, part), peers, stride=24), :] for half in range(2)
    ]
    return jnp.concatenate(halves, axis=1)


def dft_row(table, grid_rows, scale, wide, row, peers):
    total = jnp.dot(table[...], grid_rows, preferred_element_type=F32)
    for slot in range(2):
        for part in range(2):
            start = (slot * 2 + part) * peers
            for half in range(2):
                block = total[start : start + peers, half * LANES : (half + 1) * LANES]
                if scale is not None:
                    block = block * scale[slot]
                wide[pl.ds(message_row(row, half, slot, part), peers, stride=24), :] = block


def dft_kernel(grid, table, out, stage, wide):
    across, rows, lon, _ = grid.shape
    peers = out.shape[0]
    stage[...] = jnp.zeros_like(stage)
    for row in range(rows):
        for j in range(across):
            stage[row, j * ROW_PAD : j * ROW_PAD + lon, :] = grid[j, row]
        dft_row(table, stage[row], None, wide, row, peers)
    out[...] = wide[...].reshape(out.shape).astype(BF16)


def analysis_kernel(weighted, received, lat_w, folded, out, wide, columns):
    peers = received.shape[0]
    wide[...] = received[...].astype(F32).reshape(wide.shape)
    rows = received.shape[1] // 8
    for slot in range(2):
        for row in range(rows):
            start = (slot * rows + row) * peers
            for part in range(2):
                for half in range(2):
                    block = wide[
                        pl.ds(message_row(row, half, slot, part), peers, stride=24), :
                    ]
                    if weighted:
                        block = block * lat_w[row * peers : (row + 1) * peers, :]
                    lane = (part * 2 + half) * LANES
                    columns[start : start + peers, lane : lane + LANES] = block.astype(BF16)
    total = jnp.dot(folded[...], columns[...], preferred_element_type=F32).astype(BF16)
    groups = out.shape[0]
    for quarter in range(4):
        lanes = slice(quarter * LANES, (quarter + 1) * LANES)
        out[:, quarter * 16 : (quarter + 1) * 16, :] = total[:512, lanes].reshape(groups, 16, LANES)
    extra = total[512:528, :].astype(F32)
    tail = jnp.concatenate(
        [extra[0:1, q * LANES : (q + 1) * LANES] for q in range(4)]
        + [jnp.zeros((4, LANES), F32)],
        axis=0,
    )
    out[:, 64:72, :] = jnp.broadcast_to(tail.astype(BF16)[None], (groups, 8, LANES))


def synthesis_kernel(weighted, received, lat_w, spread, out, wide, degrees):
    peers = out.shape[0]
    groups = received.shape[0]
    rows = out.shape[1] // 8
    for quarter in range(4):
        lanes = slice(quarter * LANES, (quarter + 1) * LANES)
        degrees[:512, lanes] = received[:, quarter * 16 : (quarter + 1) * 16, :].reshape(512, LANES)
    tail = jnp.sum(received[...].astype(F32)[:, 64:72, :], axis=0)
    extra = jnp.concatenate([tail[q : q + 1, :] for q in range(4)], axis=1)
    first = lax.broadcasted_iota(jnp.int32, (128, 512), 0) == 0
    degrees[512:640, :] = jnp.where(first, extra, 0.0).astype(BF16)
    for slot in range(2):
        for row in range(rows):
            total = jnp.dot(
                spread[slot, row * peers : (row + 1) * peers, :],
                degrees[...],
                preferred_element_type=F32,
            )
            for part in range(2):
                for half in range(2):
                    lane = (part * 2 + half) * LANES
                    block = total[:, lane : lane + LANES]
                    if weighted:
                        block = block * lat_w[row * peers : (row + 1) * peers, :]
                    wide[pl.ds(message_row(row, half, slot, part), peers, stride=24), :] = block
    out[...] = wide[...].reshape(out.shape).astype(BF16)


def degree_rows(wide, index, groups):
    parts = []
    for part in range(2):
        halves = [
            wide[pl.ds((part * 2 + half) * 16 + index, groups, stride=72), :] for half in range(2)
        ]
        parts.append(jnp.concatenate(halves, axis=1))
    return jnp.concatenate(parts, axis=0)


def extra_rows(wide, groups):
    parts = []
    for part in range(2):
        halves = [
            wide[pl.ds(64 + part * 2 + half, groups, stride=72), :] for half in range(2)
        ]
        parts.append(jnp.concatenate(halves, axis=1))
    return jnp.concatenate(parts, axis=0)


def store_rows(wide, start_of, values, groups):
    for part in range(2):
        for half in range(2):
            wide[pl.ds(start_of(part * 2 + half), groups, stride=72), :] = values[
                part * groups : (part + 1) * groups, half * LANES : (half + 1) * LANES
            ]


def pair_masks(lowest, degree):
    partner = 511 - degree
    return (
        lowest >= 0,
        degree >= lowest,
        partner >= lowest,
        511 - lowest == degree,
        511 - lowest == partner,
    )


def filter_kernel(received, weight, lowest_ref, degrees, out, kept, wide, result):
    groups = received.shape[0]
    wide[...] = received[...].astype(F32).reshape(wide.shape)
    result[...] = jnp.zeros_like(result)
    lowest = lowest_ref[...]
    extra = extra_rows(wide, groups)
    extra_sum = jnp.zeros_like(extra)
    for index in range(8):
        mirror = 15 - index
        degree = degrees[index]
        _, near, far, extra_near, extra_far = pair_masks(lowest, degree)
        one = degree_rows(wide, index, groups)
        two = degree_rows(wide, mirror, groups)
        kept[index] = jnp.concatenate(
            [jnp.where(near, one, 0.0), jnp.where(far, 0.0, two), jnp.where(extra_near, extra, 0.0)],
            axis=0,
        ).astype(BF16)
        kept[mirror] = jnp.concatenate(
            [jnp.where(near, 0.0, one), jnp.where(far, two, 0.0), jnp.where(extra_far, extra, 0.0)],
            axis=0,
        ).astype(BF16)
        stacked = jnp.concatenate([one, two, extra], axis=0).astype(BF16)
        by_one = jnp.dot(stacked, weight[index], preferred_element_type=F32)
        by_two = jnp.dot(stacked, weight[mirror], preferred_element_type=F32)
        side = 2 * groups
        store_rows(
            wide=result,
            start_of=lambda quarter: quarter * 16 + index,
            values=jnp.where(near, by_one[:side], by_two[:side]),
            groups=groups,
        )
        store_rows(
            wide=result,
            start_of=lambda quarter: quarter * 16 + mirror,
            values=jnp.where(far, by_two[side : 2 * side], by_one[side : 2 * side]),
            groups=groups,
        )
        extra_sum = (
            extra_sum
            + jnp.where(extra_near, by_one[2 * side :], 0.0)
            + jnp.where(extra_far, by_two[2 * side :], 0.0)
        )
    store_rows(result, lambda quarter: 64 + quarter, extra_sum, groups)
    out[...] = result[...].reshape(out.shape).astype(BF16)


def filter_back_kernel(received, weight, kept, lowest_ref, degrees, out, grad_w, wide, result):
    groups = received.shape[0]
    wide[...] = received[...].astype(F32).reshape(wide.shape)
    result[...] = jnp.zeros_like(result)
    lowest = lowest_ref[...]
    extra = extra_rows(wide, groups)
    extra_sum = jnp.zeros_like(extra)
    turned = (((1,), (1,)), ((), ()))
    summed = (((0,), (0,)), ((), ()))
    for index in range(8):
        mirror = 15 - index
        degree = degrees[index]
        _, near, far, extra_near, extra_far = pair_masks(lowest, degree)
        one = degree_rows(wide, index, groups)
        two = degree_rows(wide, mirror, groups)
        stacked = jnp.concatenate([one, two, extra], axis=0).astype(BF16)
        for place in (index, mirror):
            grad_w[place] = lax.dot_general(
                kept[place], stacked, summed, preferred_element_type=F32
            ).astype(BF16)
        by_one = lax.dot_general(stacked, weight[index], turned, preferred_element_type=F32)
        by_two = lax.dot_general(stacked, weight[mirror], turned, preferred_element_type=F32)
        side = 2 * groups
        store_rows(
            wide=result,
            start_of=lambda quarter: quarter * 16 + index,
            values=jnp.where(near, by_one[:side], by_two[:side]),
            groups=groups,
        )
        store_rows(
            wide=result,
            start_of=lambda quarter: quarter * 16 + mirror,
            values=jnp.where(far, by_two[side : 2 * side], by_one[side : 2 * side]),
            groups=groups,
        )
        extra_sum = (
            extra_sum
            + jnp.where(extra_near, by_one[2 * side :], 0.0)
            + jnp.where(extra_far, by_two[2 * side :], 0.0)
        )
    store_rows(result, lambda quarter: 64 + quarter, extra_sum, groups)
    out[...] = result[...].reshape(out.shape).astype(BF16)


def idft_row(table_back, wide, scale, row, peers):
    pieces = []
    for slot in range(2):
        for part in range(2):
            halves = []
            for half in range(2):
                block = wide[pl.ds(message_row(row, half, slot, part), peers, stride=24), :]
                if scale is not None:
                    block = block * scale[slot]
                halves.append(block.astype(BF16))
            pieces.append(jnp.concatenate(halves, axis=1))
    spectrum = jnp.concatenate(pieces, axis=0)
    return jnp.dot(table_back[...], spectrum, preferred_element_type=F32)


def middle_kernel(
    received, table_back, table, scale, grid, cotangent, spectrum, output, wide, stage, linear
):
    across, rows, lon, _ = grid.shape
    peers = received.shape[0]
    wide[...] = received[...].astype(F32).reshape(wide.shape)
    stage[...] = jnp.zeros_like(stage)
    for row in range(rows):
        linear[...] = idft_row(table_back, wide, scale, row, peers)
        for j in range(across):
            value = linear[j * ROW_PAD : j * ROW_PAD + lon, :].astype(BF16).astype(F32)
            square = value * value
            bend = jnp.tanh(GELU_A * value * (1.0 + GELU_B * square))
            gate = 0.5 * (1.0 + bend)
            output[j, row] = (grid[j, row].astype(F32) + value * gate).astype(BF16)
            slope = gate + (0.5 * GELU_A) * value * (1.0 - bend * bend) * (
                1.0 + (3.0 * GELU_B) * square
            )
            stage[row, j * ROW_PAD : j * ROW_PAD + lon, :] = (
                cotangent[j, row].astype(F32) * slope
            ).astype(BF16)
    for row in range(rows):
        dft_row(table, stage[row], scale, wide, row, peers)
    spectrum[...] = wide[...].reshape(spectrum.shape).astype(BF16)


def last_kernel(received, table_back, cotangent, out, wide, linear):
    across, rows, lon, _ = cotangent.shape
    peers = received.shape[0]
    wide[...] = received[...].astype(F32).reshape(wide.shape)
    for row in range(rows):
        linear[...] = idft_row(table_back, wide, None, row, peers)
        for j in range(across):
            value = linear[j * ROW_PAD : j * ROW_PAD + lon, :].astype(BF16).astype(F32)
            out[j, row] = (cotangent[j, row].astype(F32) + value).astype(BF16)


def tables(waves, lon_count, across):
    block = lon_count // across
    place = jnp.arange(ROW_PAD, dtype=jnp.int32)[:, None]
    angle = (2.0 * math.pi / lon_count) * (place * waves[None, :] % lon_count).astype(F32)
    size = jnp.where(place < block, 1.0 / math.sqrt(lon_count), 0.0)
    cosine, sine = jnp.cos(angle) * size, jnp.sin(angle) * size
    turn = jnp.arange(across, dtype=jnp.int32)[:, None] * waves[None, :] % across
    turn = (2.0 * math.pi / across) * turn.astype(F32)
    turn_cos, turn_sin = jnp.cos(turn)[:, None, :], jnp.sin(turn)[:, None, :]
    real = (cosine * turn_cos - sine * turn_sin).astype(BF16)
    imag = -(sine * turn_cos + cosine * turn_sin).astype(BF16)
    half = waves.shape[0] // 2
    back = jnp.concatenate(
        [real[..., :half], imag[..., :half], real[..., half:], imag[..., half:]], axis=-1
    )
    return back.reshape(across * ROW_PAD, 2 * waves.shape[0])


def degree_tables(legendre, own_waves, degrees, polar_count, across):
    slots, lat_all, degree_count = legendre.shape
    rows = lat_all // (polar_count * across)
    ordered = (
        legendre.reshape(slots, polar_count, rows, across, degree_count)
        .transpose(0, 2, 1, 3, 4)
        .reshape(slots, lat_all, degree_count)
    )
    unused = jnp.full((LANES - 1,), -1, jnp.int32)
    first = jnp.concatenate([degrees, jnp.full((LANES,), -1, jnp.int32)])
    second = jnp.concatenate(
        [
            jnp.where(degrees == own_waves[0], -1, degree_count - 1 - degrees),
            own_waves[1:2],
            unused,
        ]
    )
    wanted = jnp.stack([first, second])
    chosen = (
        wanted[:, :, None] == jnp.arange(degree_count, dtype=jnp.int32)[None, None, :]
    ).astype(BF16)
    spread = jnp.einsum("sal,sil->sai", ordered, chosen, preferred_element_type=F32).astype(BF16)
    folded = jnp.concatenate(
        [
            jnp.einsum(
                "il,al->ia", chosen[s, : degree_count + 16], ordered[s], preferred_element_type=F32
            ).astype(BF16)
            for s in range(slots)
        ],
        axis=1,
    )
    return folded, spread


def body(field, cotangent, legendre, lat_weight, filter_weight, wave_order, deg_order):
    polar_count = lax.axis_size("polar")
    across = lax.axis_size("azimuth")
    peers = polar_count * across
    both = ("polar", "azimuth")
    lat_rows, lon_cols, channels = field.shape
    rows = lat_rows // across
    slots, lat_all, degree_count = legendre.shape
    block_size = degree_count // deg_order.shape[0]
    polar, azimuth = lax.axis_index("polar"), lax.axis_index("azimuth")
    device = polar * across + azimuth
    lon_count = lon_cols * across

    def to_bands(grid):
        return grid.reshape(rows, across, lon_cols, channels).transpose(1, 0, 2, 3)

    def from_bands(bands):
        return bands.transpose(1, 0, 2, 3).reshape(lat_rows, lon_cols, channels)

    partner = jnp.arange(across, dtype=jnp.int32) ^ azimuth
    trade = [[(i, i ^ k) for i in range(across)] for k in range(across)]

    def swap_bands(bands):
        chosen = jnp.take(bands, partner, axis=0)
        moved = [chosen[0]] + [
            lax.ppermute(chosen[k], "azimuth", trade[k]) for k in range(1, across)
        ]
        return moved

    def place_bands(moved):
        return jnp.take(jnp.stack(moved), partner, axis=0)

    grid = exchange(to_bands(field), "azimuth")

    pairs = wave_order.reshape(peers, slots)
    own_waves = lax.dynamic_slice_in_dim(pairs, device, 1, 0)[0]
    waves = pairs.T.reshape(-1)
    table_back = tables(waves, lon_count, across)
    table = table_back.T
    scale = jnp.broadcast_to(
        jnp.where(pairs.T == 0, 1.0, 2.0).astype(F32)[:, :, None], (slots, peers, LANES)
    )
    degrees = (
        deg_order[:, None] * block_size + jnp.arange(block_size, dtype=jnp.int32)[None, :]
    ).reshape(-1)
    folded, spread = degree_tables(legendre, own_waves, degrees, polar_count, across)
    lat_w = jnp.broadcast_to(
        lat_weight.reshape(polar_count, rows, across).transpose(1, 0, 2).reshape(-1, 1),
        (lat_all, LANES),
    )
    local_degrees = filter_weight.shape[0]
    own_degrees = lax.dynamic_slice_in_dim(degrees, polar * local_degrees, local_degrees)
    lowest = lax.dynamic_slice_in_dim(
        pairs[:, 0].reshape(polar_count, across), azimuth, 1, 1
    )
    lowest = jnp.broadcast_to(jnp.tile(lowest, (2, 1)), (2 * polar_count, channels))
    cot_bands = to_bands(cotangent)

    message = (peers, 8 * rows, LANES)
    degree_message = (polar_count, 72, LANES)
    wide = pltpu.VMEM((peers * 8 * rows, LANES), F32)
    degree_wide = pltpu.VMEM((polar_count * 72, LANES), F32)
    stage = pltpu.VMEM((rows, across * ROW_PAD, channels), BF16)
    linear = pltpu.VMEM((across * ROW_PAD, channels), F32)
    spectrum_shape = jax.ShapeDtypeStruct(message, BF16)
    degree_shape = jax.ShapeDtypeStruct(degree_message, BF16)
    band_shape = jax.ShapeDtypeStruct(grid.shape, BF16)
    smem = pl.BlockSpec(memory_space=pltpu.SMEM)

    def filter_call(kernel, second, *operands):
        vmem = pl.BlockSpec(memory_space=pltpu.VMEM)
        return pl.pallas_call(
            kernel,
            out_shape=(degree_shape, second),
            in_specs=[vmem] * (len(operands) - 1) + [smem],
            out_specs=(vmem, vmem),
            scratch_shapes=[degree_wide, degree_wide],
            compiler_params=pltpu.CompilerParams(vmem_limit_bytes=24 * MIB),
            cost_estimate=pl.CostEstimate(
                flops=500_000_000, bytes_accessed=6_000_000, transcendentals=0
            ),
        )(*operands)

    def analysis(received, weighted):
        return call(
            functools.partial(analysis_kernel, weighted),
            degree_shape,
            [wide, pltpu.VMEM((slots * lat_all, 4 * LANES), BF16)],
            24,
            800_000_000,
            5_000_000,
            received,
            lat_w,
            folded,
        )

    def synthesis(received, weighted):
        return call(
            functools.partial(synthesis_kernel, weighted),
            spectrum_shape,
            [wide, pltpu.VMEM((640, 4 * LANES), BF16)],
            24,
            800_000_000,
            5_000_000,
            received,
            lat_w,
            spread,
        )

    spectrum = call(
        dft_kernel, spectrum_shape, [stage, wide], 28, 2_400_000_000, 8_000_000, grid, table
    )
    spectrum, cot_bands = lax.optimization_barrier((spectrum, cot_bands))
    cot_moved = swap_bands(cot_bands)
    arrived = exchange(spectrum, both)
    arrived, cot_moved = lax.optimization_barrier((arrived, cot_moved))
    cot_grid = place_bands(cot_moved)

    coeffs = exchange(analysis(arrived, True), "polar")
    filtered, kept = filter_call(
        filter_kernel,
        jax.ShapeDtypeStruct((local_degrees, 6 * polar_count, channels), BF16),
        coeffs,
        filter_weight,
        lowest,
        own_degrees,
    )
    grid_spec = synthesis(exchange(filtered, "polar"), False)
    arrived = exchange(grid_spec, both)
    grad_spec, output_bands = call(
        middle_kernel,
        (spectrum_shape, band_shape),
        [wide, stage, linear],
        40,
        4_800_000_000,
        16_000_000,
        arrived,
        table_back,
        table,
        scale,
        grid,
        cot_grid,
    )
    grad_spec, output_bands = lax.optimization_barrier((grad_spec, output_bands))
    output_moved = swap_bands(output_bands)
    arrived = exchange(grad_spec, both)
    arrived, output_moved = lax.optimization_barrier((arrived, output_moved))
    output = from_bands(place_bands(output_moved))

    grad_filtered = exchange(analysis(arrived, False), "polar")
    grad_coeffs, weight_terms = filter_call(
        filter_back_kernel,
        jax.ShapeDtypeStruct(filter_weight.shape, BF16),
        grad_filtered,
        filter_weight,
        kept,
        lowest,
        own_degrees,
    )
    grad_weight = lax.psum_scatter(
        weight_terms, "azimuth", scatter_dimension=1, tiled=True
    ).astype(F32)
    grad_weighted = synthesis(exchange(grad_coeffs, "polar"), True)
    arrived = exchange(grad_weighted, both)
    grad_bands = call(
        last_kernel,
        band_shape,
        [wide, linear],
        28,
        2_400_000_000,
        8_000_000,
        arrived,
        table_back,
        cot_grid,
    )
    grad_field = from_bands(exchange(grad_bands, "azimuth"))
    return (output, grad_field, grad_weight)


def solution(mesh):
    placed = (
        P("polar", "azimuth", None),
        P("polar", "azimuth", None),
        P(("polar", "azimuth"), None, None),
        P(),
        P("polar", None, None),
        P(),
        P(),
    )
    return jax.shard_map(
        body,
        mesh=mesh,
        in_specs=placed,
        out_specs=(
            P("polar", "azimuth", None),
            P("polar", "azimuth", None),
            P("polar", "azimuth", None),
        ),
        check_vma=False,
    )
```

```python
import functools
import math

import jax
import jax.numpy as jnp
from jax import lax
from jax.experimental import pallas as pl
from jax.experimental.pallas import tpu as pltpu
from jax.sharding import PartitionSpec as P

BF16 = jnp.bfloat16
F32 = jnp.float32
LANES = 128
ROW_PAD = 192
MIB = 1024 * 1024
WHOLE = 56
GELU_A = math.sqrt(2.0 / math.pi)
GELU_B = 0.044715


def exchange(payload, axes):
    return lax.all_to_all(payload, axes, split_axis=0, concat_axis=0, tiled=True)


def message_row(row, half, slot, part):
    return row * 8 + half * 4 + slot * 2 + part


def unpack_rows(received, wide, row, slot, part, peers):
    halves = [
        wide[pl.ds(message_row(row, half, slot, part), peers, stride=24), :] for half in range(2)
    ]
    return jnp.concatenate(halves, axis=1)


def doubling(zero_at, slot, peers):
    place = slot * peers + lax.broadcasted_iota(jnp.int32, (peers, LANES), 0)
    return jnp.where(place == zero_at, 1.0, 2.0)


def clear_pads(stage, across, lon):
    start = lon // 16 * 16
    for j in range(across):
        stage[j * ROW_PAD + start : (j + 1) * ROW_PAD, :] = jnp.zeros(
            (ROW_PAD - start, stage.shape[1]), BF16
        )


def dft_row(table, grid_rows, zero_at, wide, row, peers):
    total = jnp.dot(table[...], grid_rows[...], preferred_element_type=F32)
    for slot in range(2):
        for part in range(2):
            start = (slot * 2 + part) * peers
            for half in range(2):
                block = total[start : start + peers, half * LANES : (half + 1) * LANES]
                if zero_at is not None:
                    block = block * doubling(zero_at, slot, peers)
                wide[pl.ds(message_row(row, half, slot, part), peers, stride=24), :] = block


def dft_kernel(grid, table_back, out, wide, table, stages):
    across, rows, lon, _ = grid.shape
    peers = out.shape[0]
    table[...] = table_back[...].T
    for row in range(rows):
        stage = stages.at[row]
        clear_pads(stage, across, lon)
        for j in range(across):
            stage[j * ROW_PAD : j * ROW_PAD + lon, :] = grid[j, row]
        dft_row(table, stage, None, wide, row, peers)
    out[...] = wide[...].reshape(out.shape).astype(BF16)


def analysis_kernel(weighted, received, lat_w, folded_far, out, wide, columns, folded, arrival):
    fetch = pltpu.make_async_copy(folded_far, folded, arrival)
    fetch.start()
    peers = received.shape[0]
    wide[...] = received[...].astype(F32).reshape(wide.shape)
    rows = received.shape[1] // 8
    for slot in range(2):
        for row in range(rows):
            start = (slot * rows + row) * peers
            for part in range(2):
                for half in range(2):
                    block = wide[
                        pl.ds(message_row(row, half, slot, part), peers, stride=24), :
                    ]
                    if weighted:
                        block = block * lat_w[row * peers : (row + 1) * peers, :]
                    lane = (part * 2 + half) * LANES
                    columns[start : start + peers, lane : lane + LANES] = block.astype(BF16)
    fetch.wait()
    total = jnp.dot(folded[...], columns[...], preferred_element_type=F32).astype(BF16)
    groups = out.shape[0]
    for quarter in range(4):
        lanes = slice(quarter * LANES, (quarter + 1) * LANES)
        out[:, quarter * 16 : (quarter + 1) * 16, :] = total[:512, lanes].reshape(groups, 16, LANES)
    extra = total[512:528, :].astype(F32)
    tail = jnp.concatenate(
        [extra[0:1, q * LANES : (q + 1) * LANES] for q in range(4)]
        + [jnp.zeros((4, LANES), F32)],
        axis=0,
    )
    out[:, 64:72, :] = jnp.broadcast_to(tail.astype(BF16)[None], (groups, 8, LANES))


def synthesis_kernel(weighted, received, lat_w, spread, out, wide, degrees):
    peers = out.shape[0]
    groups = received.shape[0]
    rows = out.shape[1] // 8
    for quarter in range(4):
        lanes = slice(quarter * LANES, (quarter + 1) * LANES)
        degrees[:512, lanes] = received[:, quarter * 16 : (quarter + 1) * 16, :].reshape(512, LANES)
    tail = jnp.sum(received[...].astype(F32)[:, 64:72, :], axis=0)
    extra = jnp.concatenate([tail[q : q + 1, :] for q in range(4)], axis=1)
    first = lax.broadcasted_iota(jnp.int32, (128, 512), 0) == 0
    degrees[512:640, :] = jnp.where(first, extra, 0.0).astype(BF16)
    for slot in range(2):
        for row in range(rows):
            total = jnp.dot(
                spread[slot, row * peers : (row + 1) * peers, :],
                degrees[...],
                preferred_element_type=F32,
            )
            for part in range(2):
                for half in range(2):
                    lane = (part * 2 + half) * LANES
                    block = total[:, lane : lane + LANES]
                    if weighted:
                        block = block * lat_w[row * peers : (row + 1) * peers, :]
                    wide[pl.ds(message_row(row, half, slot, part), peers, stride=24), :] = block
    out[...] = wide[...].reshape(out.shape).astype(BF16)


def degree_rows(wide, index, groups):
    parts = []
    for part in range(2):
        halves = [
            wide[pl.ds((part * 2 + half) * 16 + index, groups, stride=72), :] for half in range(2)
        ]
        parts.append(jnp.concatenate(halves, axis=1))
    return jnp.concatenate(parts, axis=0)


def extra_rows(wide, groups):
    parts = []
    for part in range(2):
        halves = [
            wide[pl.ds(64 + part * 2 + half, groups, stride=72), :] for half in range(2)
        ]
        parts.append(jnp.concatenate(halves, axis=1))
    return jnp.concatenate(parts, axis=0)


def store_rows(wide, start_of, values, groups):
    for part in range(2):
        for half in range(2):
            wide[pl.ds(start_of(part * 2 + half), groups, stride=72), :] = values[
                part * groups : (part + 1) * groups, half * LANES : (half + 1) * LANES
            ]


def pair_masks(lowest, degree):
    partner = 511 - degree
    return (
        lowest >= 0,
        degree >= lowest,
        partner >= lowest,
        511 - lowest == degree,
        511 - lowest == partner,
    )


def lowest_waves(own, first, shape):
    column = lax.broadcasted_iota(jnp.int32, first.shape, 1) == own[0]
    lowest = jnp.sum(jnp.where(column, first[...], 0), axis=1, keepdims=True)
    return jnp.broadcast_to(jnp.concatenate([lowest, lowest], axis=0), shape)


def filter_kernel(own, blocks, received, weight, first, out, wide, result):
    groups = received.shape[0]
    wide[...] = received[...].astype(F32).reshape(wide.shape)
    result[...] = jnp.zeros_like(result)
    extra = extra_rows(wide, groups)
    lowest = lowest_waves(own, first, extra.shape)
    extra_sum = jnp.zeros_like(extra)
    for index in range(8):
        mirror = 15 - index
        degree = blocks[2 * own[1]] * 8 + index
        _, near, far, extra_near, extra_far = pair_masks(lowest, degree)
        one = degree_rows(wide, index, groups)
        two = degree_rows(wide, mirror, groups)
        stacked = jnp.concatenate([one, two, extra], axis=0).astype(BF16)
        by_one = jnp.dot(stacked, weight[index], preferred_element_type=F32)
        by_two = jnp.dot(stacked, weight[mirror], preferred_element_type=F32)
        side = 2 * groups
        store_rows(
            wide=result,
            start_of=lambda quarter: quarter * 16 + index,
            values=jnp.where(near, by_one[:side], by_two[:side]),
            groups=groups,
        )
        store_rows(
            wide=result,
            start_of=lambda quarter: quarter * 16 + mirror,
            values=jnp.where(far, by_two[side : 2 * side], by_one[side : 2 * side]),
            groups=groups,
        )
        extra_sum = (
            extra_sum
            + jnp.where(extra_near, by_one[2 * side :], 0.0)
            + jnp.where(extra_far, by_two[2 * side :], 0.0)
        )
    store_rows(result, lambda quarter: 64 + quarter, extra_sum, groups)
    out[...] = result[...].reshape(out.shape).astype(BF16)


def filter_back_kernel(
    own, blocks, received, weight, first, coeffs, out, grad_w, wide, result, wide_coeffs
):
    groups = received.shape[0]
    wide[...] = received[...].astype(F32).reshape(wide.shape)
    wide_coeffs[...] = coeffs[...].astype(F32).reshape(wide.shape)
    result[...] = jnp.zeros_like(result)
    extra = extra_rows(wide, groups)
    lowest = lowest_waves(own, first, extra.shape)
    extra_sum = jnp.zeros_like(extra)
    kept_extra = extra_rows(wide_coeffs, groups)
    turned = (((1,), (1,)), ((), ()))
    summed = (((0,), (0,)), ((), ()))
    for index in range(8):
        mirror = 15 - index
        degree = blocks[2 * own[1]] * 8 + index
        _, near, far, extra_near, extra_far = pair_masks(lowest, degree)
        one = degree_rows(wide, index, groups)
        two = degree_rows(wide, mirror, groups)
        stacked = jnp.concatenate([one, two, extra], axis=0).astype(BF16)
        kept_one = degree_rows(wide_coeffs, index, groups)
        kept_two = degree_rows(wide_coeffs, mirror, groups)
        kept_near = jnp.concatenate(
            [
                jnp.where(near, kept_one, 0.0),
                jnp.where(far, 0.0, kept_two),
                jnp.where(extra_near, kept_extra, 0.0),
            ],
            axis=0,
        ).astype(BF16)
        kept_far = jnp.concatenate(
            [
                jnp.where(near, 0.0, kept_one),
                jnp.where(far, kept_two, 0.0),
                jnp.where(extra_far, kept_extra, 0.0),
            ],
            axis=0,
        ).astype(BF16)
        for place, kept in ((index, kept_near), (mirror, kept_far)):
            grad_w[place] = lax.dot_general(
                kept, stacked, summed, preferred_element_type=F32
            ).astype(BF16)
        by_one = lax.dot_general(stacked, weight[index], turned, preferred_element_type=F32)
        by_two = lax.dot_general(stacked, weight[mirror], turned, preferred_element_type=F32)
        side = 2 * groups
        store_rows(
            wide=result,
            start_of=lambda quarter: quarter * 16 + index,
            values=jnp.where(near, by_one[:side], by_two[:side]),
            groups=groups,
        )
        store_rows(
            wide=result,
            start_of=lambda quarter: quarter * 16 + mirror,
            values=jnp.where(far, by_two[side : 2 * side], by_one[side : 2 * side]),
            groups=groups,
        )
        extra_sum = (
            extra_sum
            + jnp.where(extra_near, by_one[2 * side :], 0.0)
            + jnp.where(extra_far, by_two[2 * side :], 0.0)
        )
    store_rows(result, lambda quarter: 64 + quarter, extra_sum, groups)
    out[...] = result[...].reshape(out.shape).astype(BF16)


def idft_row(table_back, wide, zero_at, row, peers, linear):
    pieces = []
    for slot in range(2):
        for part in range(2):
            halves = []
            for half in range(2):
                block = wide[pl.ds(message_row(row, half, slot, part), peers, stride=24), :]
                if zero_at is not None:
                    block = block * doubling(zero_at, slot, peers)
                halves.append(block.astype(BF16))
            pieces.append(jnp.concatenate(halves, axis=1))
    spectrum = jnp.concatenate(pieces, axis=0)
    linear[...] = jnp.dot(table_back[...], spectrum, preferred_element_type=F32)


def middle_kernel(own, received, table_back, grid_far, *refs):
    across, rows, lon, _ = grid_far.shape
    cot_far, spectrum, out_far = refs[:across], refs[across], refs[across + 1]
    wide, table, grid, cotangent, output, stages, linears = refs[across + 2 : across + 9]
    grid_in, cot_in, leaving = refs[across + 9 :]
    others = [pltpu.make_async_copy(grid_far, grid, grid_in)] + [
        pltpu.make_async_copy(cot_far[k], cotangent.at[own[0] ^ k], cot_in.at[k])
        for k in range(across)
    ]
    for copy in others:
        copy.start()
    zero_at = own[2]
    peers = received.shape[0]
    wide[...] = received[...].astype(F32).reshape(wide.shape)
    for row in range(rows):
        clear_pads(stages.at[row], across, lon)
        idft_row(table_back, wide, zero_at, row, peers, linears.at[row])
    table[...] = table_back[...].T
    for copy in others:
        copy.wait()
    leave = [
        pltpu.make_async_copy(output.at[row], out_far.at[:, row], leaving.at[row])
        for row in range(rows)
    ]
    for row in range(rows):
        linear, stage = linears.at[row], stages.at[row]
        for j in range(across):
            place = slice(j * ROW_PAD, j * ROW_PAD + lon)
            value = linear[place, :].astype(BF16).astype(F32)
            square = value * value
            bend = jnp.tanh(value * (GELU_A + (GELU_A * GELU_B) * square))
            gate = 0.5 + 0.5 * bend
            output[row, j] = (grid[j, row].astype(F32) + value * gate).astype(BF16)
            steep = value * (2.0 * GELU_A + (6.0 * GELU_A * GELU_B) * square)
            slope = gate + steep * (gate - gate * gate)
            stage[place, :] = (cotangent[j, row].astype(F32) * slope).astype(BF16)
        leave[row].start()
        dft_row(table, stage, zero_at, wide, row, peers)
    spectrum[...] = wide[...].reshape(spectrum.shape).astype(BF16)
    for copy in leave:
        copy.wait()


def last_kernel(own, received, table_back, *refs):
    across = len(refs) - 7
    cot_far, out_far = refs[:across], refs[across]
    wide, cotangent, output, linears, cot_in, leaving = refs[across + 1 :]
    _, rows, lon, _ = out_far.shape
    others = [
        pltpu.make_async_copy(cot_far[k], cotangent.at[own[0] ^ k], cot_in.at[k])
        for k in range(across)
    ]
    for copy in others:
        copy.start()
    peers = received.shape[0]
    wide[...] = received[...].astype(F32).reshape(wide.shape)
    leave = [
        pltpu.make_async_copy(output.at[row], out_far.at[:, row], leaving.at[row])
        for row in range(rows)
    ]
    for row in range(rows):
        linear = linears.at[row]
        idft_row(table_back, wide, None, row, peers, linear)
        if row == 0:
            for copy in others:
                copy.wait()
        for j in range(across):
            value = linear[j * ROW_PAD : j * ROW_PAD + lon, :].astype(BF16).astype(F32)
            output[row, j] = (cotangent[j, row].astype(F32) + value).astype(BF16)
        leave[row].start()
    for copy in leave:
        copy.wait()


def split_kernel(grid, *refs):
    lon, lat, _ = grid.shape
    wide = refs[-1]
    wide[...] = grid[...].astype(F32).reshape(wide.shape)
    across, rows = refs[0].shape[:2]
    for j in range(across):
        for row in range(rows):
            refs[0][j, row] = wide[pl.ds(row * across + j, lon, stride=lat), :].astype(BF16)


def split_far_kernel(own, grid, *refs):
    lon, lat, channels = grid.shape
    across = len(refs) - 3
    outs, (wide, bands, leaving) = refs[:across], refs[across:]
    rows = outs[0].shape[0]
    for lane in range(0, channels, LANES):
        lanes = slice(lane, lane + LANES)
        wide[...] = grid[:, :, lanes].astype(F32).reshape(wide.shape)
        for k in range(across):
            for row in range(rows):
                start = row * across + (own[0] ^ k)
                bands[k, row, :, lanes] = wide[pl.ds(start, lon, stride=lat), :].astype(BF16)
    copies = [
        pltpu.make_async_copy(bands.at[k], outs[k], leaving.at[k]) for k in range(across)
    ]
    for copy in copies:
        copy.start()
    for copy in copies:
        copy.wait()


def join_kernel(own, *refs):
    bands, out, wide = refs[:-2], refs[-2], refs[-1]
    lon, lat, _ = out.shape
    across, rows = len(bands), bands[0].shape[0]
    for k in range(across):
        for row in range(rows):
            start = row * across + (own[0] ^ k)
            wide[pl.ds(start, lon, stride=lat), :] = bands[k][row].astype(F32)
    out[...] = wide[...].reshape(out.shape).astype(BF16)


def degree_tables_kernel(own, blocks, waves, legendre, folded, spread, ordered, chosen):
    slots, lat_all, degree_count = legendre.shape
    count = degree_count // 16
    own_waves = [waves[own[3] * slots + slot] for slot in range(slots)]
    step = lax.broadcasted_iota(jnp.int32, (8, degree_count), 0)
    lane = lax.broadcasted_iota(jnp.int32, (8, degree_count), 1)
    chosen[...] = jnp.zeros_like(chosen)
    for pair in range(count):
        for slot in range(slots):
            pieces = []
            for block in (2 * pair, 2 * pair + 1):
                degree = blocks[block] * 8 + step
                if slot:
                    degree = jnp.where(
                        degree == own_waves[0], degree_count, degree_count - 1 - degree
                    )
                pieces.append(jnp.where(degree == lane, 1.0, 0.0))
            chosen[slot, pair * 16 : (pair + 1) * 16, :] = jnp.concatenate(pieces, axis=0).astype(
                BF16
            )
    sixteen = lax.broadcasted_iota(jnp.int32, (16, degree_count), 0)
    lanes = lax.broadcasted_iota(jnp.int32, (16, degree_count), 1)
    last = jnp.where(jnp.logical_and(sixteen == 0, lanes == own_waves[1]), 1.0, 0.0)
    chosen[1, degree_count : degree_count + 16, :] = last.astype(BF16)
    turned = (((1,), (1,)), ((), ()))
    for slot in range(slots):
        plane = legendre[slot].astype(F32).reshape(-1, lat_all // 256, 8, degree_count)
        for row in range(lat_all // 256):
            ordered[row * 256 : (row + 1) * 256, :] = (
                plane[:, row].reshape(256, degree_count).astype(BF16)
            )
        spread[slot] = lax.dot_general(
            ordered[...], chosen[slot], turned, preferred_element_type=F32
        ).astype(BF16)
        folded[:, slot * lat_all : (slot + 1) * lat_all] = lax.dot_general(
            chosen[slot, : degree_count + 16, :], ordered[...], turned, preferred_element_type=F32
        ).astype(BF16)


def tables(waves, lon_count, across):
    block = lon_count // across
    place = jnp.arange(ROW_PAD, dtype=jnp.int32)[:, None]
    angle = (2.0 * math.pi / lon_count) * (place * waves[None, :] % lon_count).astype(F32)
    size = jnp.where(place < block, 1.0 / math.sqrt(lon_count), 0.0)
    cosine, sine = jnp.cos(angle) * size, jnp.sin(angle) * size
    turn = jnp.arange(across, dtype=jnp.int32)[:, None] * waves[None, :] % across
    turn = (2.0 * math.pi / across) * turn.astype(F32)
    turn_cos, turn_sin = jnp.cos(turn)[:, None, :], jnp.sin(turn)[:, None, :]
    real = (cosine * turn_cos - sine * turn_sin).astype(BF16)
    imag = -(sine * turn_cos + cosine * turn_sin).astype(BF16)
    half = waves.shape[0] // 2
    back = jnp.concatenate(
        [real[..., :half], imag[..., :half], real[..., half:], imag[..., half:]], axis=-1
    )
    return back.reshape(across * ROW_PAD, 2 * waves.shape[0])


def body(field, cotangent, legendre, lat_weight, filter_weight, wave_order, deg_order):
    polar_count = lax.axis_size("polar")
    across = lax.axis_size("azimuth")
    peers = polar_count * across
    both = ("polar", "azimuth")
    lat_rows, lon_cols, channels = field.shape
    rows = lat_rows // across
    slots, lat_all, degree_count = legendre.shape
    block_size = degree_count // deg_order.shape[0]
    polar, azimuth = lax.axis_index("polar"), lax.axis_index("azimuth")
    device = polar * across + azimuth
    lon_count = lon_cols * across

    vmem = pl.BlockSpec(memory_space=pltpu.VMEM)
    smem = pl.BlockSpec(memory_space=pltpu.SMEM)
    far = pl.BlockSpec(memory_space=pltpu.HBM)
    pairs = wave_order.reshape(peers, slots)
    waves = pairs.T.reshape(-1)
    zero_at = jnp.sum(jnp.where(waves == 0, jnp.arange(waves.shape[0], dtype=jnp.int32), 0))
    own = jnp.stack([azimuth, polar, zero_at, device])
    band = (rows, lon_cols, channels)
    bands_shape = (across, *band)
    one_band = jax.ShapeDtypeStruct(band, BF16)
    trade = [[(i, i ^ k) for i in range(across)] for k in range(across)]

    def kernel_call(kernel, outs, in_specs, out_specs, scratch, mib, cost, *operands):
        return pl.pallas_call(
            kernel,
            out_shape=outs,
            in_specs=in_specs,
            out_specs=out_specs,
            scratch_shapes=scratch,
            compiler_params=pltpu.CompilerParams(vmem_limit_bytes=mib * MIB),
            cost_estimate=pl.CostEstimate(
                flops=cost, bytes_accessed=cost // 1000, transcendentals=0
            ),
        )(*operands)

    def half_bands(kernel, ins, outs, scalars, *operands):
        def spec(array):
            inner = tuple(array.shape[:-1])
            return pl.BlockSpec((*inner, LANES), lambda h: (0,) * len(inner) + (h,))

        return pl.pallas_call(
            kernel,
            grid=(channels // LANES,),
            out_shape=outs,
            in_specs=[smem] * len(scalars) + [spec(x) for x in ins],
            out_specs=jax.tree.map(spec, outs),
            scratch_shapes=[pltpu.VMEM((lon_cols * lat_rows, LANES), F32)],
            compiler_params=pltpu.CompilerParams(vmem_limit_bytes=56 * MIB),
            cost_estimate=pl.CostEstimate(flops=2_000, bytes_accessed=2_000, transcendentals=0),
        )(*scalars, *operands)

    def join_bands(bands):
        out = jax.ShapeDtypeStruct((lon_cols, lat_rows, channels), BF16)
        return jnp.transpose(half_bands(join_kernel, bands, out, [own], *bands), (1, 0, 2))

    def piece(bands, k):
        if isinstance(bands, (list, tuple)):
            return bands[k]
        return lax.dynamic_index_in_dim(bands, azimuth ^ k, 0, keepdims=False)

    def beside(payload, axes, bands, kinds, done):
        payload, bands = lax.optimization_barrier((payload, bands))
        moved = [lax.ppermute(piece(bands, k), "azimuth", trade[k]) for k in kinds]
        payload = exchange(payload, axes)
        payload, bands, moved = lax.optimization_barrier((payload, bands, moved))
        done.update(zip(kinds, moved))
        return payload, bands

    groups = ((2, 6, 4), (1, 3, 7, 5))

    turned_field = jnp.transpose(field, (1, 0, 2))
    grid = exchange(
        half_bands(
            split_kernel,
            [turned_field],
            jax.ShapeDtypeStruct(bands_shape, BF16),
            [],
            turned_field,
        ),
        "azimuth",
    )

    table_back = tables(waves, lon_count, across)
    folded, spread = kernel_call(
        degree_tables_kernel,
        (
            jax.ShapeDtypeStruct((degree_count + 16, slots * lat_all), BF16),
            jax.ShapeDtypeStruct((slots, lat_all, degree_count + LANES), BF16),
        ),
        [smem, smem, smem, vmem],
        (vmem, vmem),
        [
            pltpu.VMEM((lat_all, degree_count), BF16),
            pltpu.VMEM((slots, degree_count + LANES, degree_count), BF16),
        ],
        32,
        1000,
        own,
        deg_order,
        wave_order,
        legendre,
    )
    lat_w = jnp.broadcast_to(
        lat_weight.reshape(polar_count, rows, across).transpose(1, 0, 2).reshape(-1, 1),
        (lat_all, LANES),
    )
    first = pairs[:, 0].reshape(polar_count, across)
    cot_send = kernel_call(
        split_far_kernel,
        (one_band,) * across,
        [smem, vmem],
        (far,) * across,
        [
            pltpu.VMEM((lon_cols * lat_rows, LANES), F32),
            pltpu.VMEM(bands_shape, BF16),
            pltpu.SemaphoreType.DMA((across,)),
        ],
        24,
        1000,
        own,
        jnp.transpose(cotangent, (1, 0, 2)),
    )
    grid, table_back, folded, spread, lat_w, first, cot_send = lax.optimization_barrier(
        (grid, table_back, folded, spread, lat_w, first, cot_send)
    )

    message = (peers, 8 * rows, LANES)
    degree_message = (polar_count, 72, LANES)
    wide = pltpu.VMEM((peers * 8 * rows, LANES), F32)
    degree_wide = pltpu.VMEM((polar_count * 72, LANES), F32)
    stages = pltpu.VMEM((rows, across * ROW_PAD, channels), BF16)
    linears = pltpu.VMEM((rows, across * ROW_PAD, channels), F32)
    held_bands = pltpu.VMEM(bands_shape, BF16)
    held_rows = pltpu.VMEM((rows, across, lon_cols, channels), BF16)
    sems = pltpu.SemaphoreType.DMA
    held_table = pltpu.VMEM(table_back.shape[::-1], BF16)
    spectrum_shape = jax.ShapeDtypeStruct(message, BF16)
    degree_shape = jax.ShapeDtypeStruct(degree_message, BF16)
    local_degrees = filter_weight.shape[0]

    def analysis(received, weighted):
        return kernel_call(
            functools.partial(analysis_kernel, weighted),
            degree_shape,
            [vmem, vmem, far],
            vmem,
            [
                wide,
                pltpu.VMEM((slots * lat_all, 4 * LANES), BF16),
                pltpu.VMEM(folded.shape, BF16),
                sems,
            ],
            24,
            800_000_000,
            received,
            lat_w,
            folded,
        )

    def synthesis(received, weighted):
        return kernel_call(
            functools.partial(synthesis_kernel, weighted),
            spectrum_shape,
            [vmem] * 3,
            vmem,
            [wide, pltpu.VMEM((degree_count + LANES, 4 * LANES), BF16)],
            24,
            800_000_000,
            received,
            lat_w,
            spread,
        )

    spectrum = kernel_call(
        dft_kernel,
        spectrum_shape,
        [vmem, vmem],
        vmem,
        [wide, held_table, stages],
        WHOLE,
        2_400_000_000,
        grid,
        table_back,
    )
    cot_bands = {0: cot_send[0]}
    arrived, cot_send = beside(spectrum, both, cot_send, groups[0], cot_bands)
    coeffs = analysis(arrived, True)
    coeffs, cot_send = beside(coeffs, "polar", cot_send, groups[1], cot_bands)
    filtered = kernel_call(
        filter_kernel,
        degree_shape,
        [smem, smem, vmem, vmem, vmem],
        vmem,
        [degree_wide, degree_wide],
        24,
        300_000_000,
        own,
        deg_order,
        coeffs,
        filter_weight,
        first,
    )
    filtered = exchange(filtered, "polar")
    cot_bands = [cot_bands[k] for k in range(across)]
    arrived = exchange(synthesis(filtered, False), both)
    grad_spec, output_bands = kernel_call(
        middle_kernel,
        (spectrum_shape, jax.ShapeDtypeStruct(bands_shape, BF16)),
        [smem, vmem, vmem] + [far] * (1 + across),
        (vmem, far),
        [
            wide,
            held_table,
            held_bands,
            held_bands,
            held_rows,
            stages,
            linears,
            sems,
            sems((across,)),
            sems((rows,)),
        ],
        WHOLE,
        4_800_000_000,
        own,
        arrived,
        table_back,
        grid,
        *cot_bands,
    )
    output_moved = {}
    arrived, output_bands = beside(grad_spec, both, output_bands, groups[0], output_moved)
    grad_filtered = analysis(arrived, False)
    grad_filtered, output_bands = beside(
        grad_filtered, "polar", output_bands, groups[1], output_moved
    )
    grad_coeffs, weight_terms = kernel_call(
        filter_back_kernel,
        (degree_shape, jax.ShapeDtypeStruct(filter_weight.shape, BF16)),
        [smem, smem, vmem, vmem, vmem, vmem],
        (vmem, vmem),
        [degree_wide, degree_wide, degree_wide],
        24,
        600_000_000,
        own,
        deg_order,
        grad_filtered,
        filter_weight,
        first,
        coeffs,
    )
    grad_coeffs = exchange(grad_coeffs, "polar")
    output_moved[0] = piece(output_bands, 0)
    grad_weight = lax.psum_scatter(
        weight_terms, "azimuth", scatter_dimension=1, tiled=True
    ).astype(F32)
    arrived = exchange(synthesis(grad_coeffs, True), both)
    grad_bands = kernel_call(
        last_kernel,
        jax.ShapeDtypeStruct(bands_shape, BF16),
        [smem, vmem, vmem] + [far] * across,
        far,
        [wide, held_bands, held_rows, linears, sems((across,)), sems((rows,))],
        WHOLE,
        2_400_000_000,
        own,
        arrived,
        table_back,
        *cot_bands,
    )
    output_moved = [output_moved[k] for k in range(across)]
    grad_bands, output_moved = lax.optimization_barrier((grad_bands, output_moved))
    output = join_bands(output_moved)
    grad_field = (
        exchange(grad_bands, "azimuth")
        .transpose(1, 0, 2, 3)
        .reshape(lat_rows, lon_cols, channels)
    )
    return (output, grad_field, grad_weight)


def solution(mesh):
    placed = (
        P("polar", "azimuth", None),
        P("polar", "azimuth", None),
        P(("polar", "azimuth"), None, None),
        P(),
        P("polar", None, None),
        P(),
        P(),
    )
    return jax.shard_map(
        body,
        mesh=mesh,
        in_specs=placed,
        out_specs=(
            P("polar", "azimuth", None),
            P("polar", "azimuth", None),
            P("polar", "azimuth", None),
        ),
        check_vma=False,
    )
```

```python
import functools
import math

import jax
import jax.numpy as jnp
from jax import lax
from jax.experimental import pallas as pl
from jax.experimental.pallas import tpu as pltpu
from jax.sharding import PartitionSpec as P

BF16 = jnp.bfloat16
F32 = jnp.float32
LANES = 128
ROW_PAD = 192
MIB = 1024 * 1024
WHOLE = 56
APART = 56
PIECES = 4
GELU_A = math.sqrt(2.0 / math.pi)
GELU_B = 0.044715


def exchange(payload, axes):
    return lax.all_to_all(payload, axes, split_axis=0, concat_axis=0, tiled=True)


def message_row(row, half, slot, part):
    return row * 8 + half * 4 + slot * 2 + part


def unpack_rows(received, wide, row, slot, part, peers):
    halves = [
        wide[pl.ds(message_row(row, half, slot, part), peers, stride=24), :] for half in range(2)
    ]
    return jnp.concatenate(halves, axis=1)


def doubling(zero_at, slot, peers):
    place = slot * peers + lax.broadcasted_iota(jnp.int32, (peers, LANES), 0)
    return jnp.where(place == zero_at, 1.0, 2.0)


def clear_pads(stage, across, lon):
    start = lon // 16 * 16
    for j in range(across):
        stage[j * ROW_PAD + start : (j + 1) * ROW_PAD, :] = jnp.zeros(
            (ROW_PAD - start, stage.shape[1]), BF16
        )


def dft_row(table, grid_rows, zero_at, wide, row, peers):
    total = jnp.dot(table[...], grid_rows[...], preferred_element_type=F32)
    for slot in range(2):
        for part in range(2):
            start = (slot * 2 + part) * peers
            for half in range(2):
                block = total[start : start + peers, half * LANES : (half + 1) * LANES]
                if zero_at is not None:
                    block = block * doubling(zero_at, slot, peers)
                wide[pl.ds(message_row(row, half, slot, part), peers, stride=24), :] = block


def dft_kernel(grid, table_back, out, wide, table, stages):
    across, rows, lon, _ = grid.shape
    peers = out.shape[0]
    table[...] = table_back[...].T
    for row in range(rows):
        stage = stages.at[row]
        clear_pads(stage, across, lon)
        for j in range(across):
            stage[j * ROW_PAD : j * ROW_PAD + lon, :] = grid[j, row]
        dft_row(table, stage, None, wide, row, peers)
    out[...] = wide[...].reshape(out.shape).astype(BF16)


def analysis_kernel(weighted, received, lat_w, folded_far, out, wide, columns, folded, arrival):
    size = folded.shape[0] // PIECES
    fetches = [
        pltpu.make_async_copy(
            folded_far.at[pl.ds(c * size, size)], folded.at[pl.ds(c * size, size)], arrival.at[c]
        )
        for c in range(PIECES)
    ]
    for fetch in fetches:
        fetch.start()
    peers = received.shape[0]
    wide[...] = received[...].astype(F32).reshape(wide.shape)
    rows = received.shape[1] // 8
    for slot in range(2):
        for row in range(rows):
            start = (slot * rows + row) * peers
            for part in range(2):
                for half in range(2):
                    block = wide[
                        pl.ds(message_row(row, half, slot, part), peers, stride=24), :
                    ]
                    if weighted:
                        block = block * lat_w[row * peers : (row + 1) * peers, :]
                    lane = (part * 2 + half) * LANES
                    columns[start : start + peers, lane : lane + LANES] = block.astype(BF16)
    for fetch in fetches:
        fetch.wait()
    total = jnp.dot(folded[...], columns[...], preferred_element_type=F32).astype(BF16)
    groups = out.shape[0]
    for quarter in range(4):
        lanes = slice(quarter * LANES, (quarter + 1) * LANES)
        out[:, quarter * 16 : (quarter + 1) * 16, :] = total[:512, lanes].reshape(groups, 16, LANES)
    extra = total[512:528, :].astype(F32)
    tail = jnp.concatenate(
        [extra[0:1, q * LANES : (q + 1) * LANES] for q in range(4)]
        + [jnp.zeros((4, LANES), F32)],
        axis=0,
    )
    out[:, 64:72, :] = jnp.broadcast_to(tail.astype(BF16)[None], (groups, 8, LANES))


def synthesis_kernel(weighted, received, lat_w, spread, out, wide, degrees):
    peers = out.shape[0]
    groups = received.shape[0]
    rows = out.shape[1] // 8
    for quarter in range(4):
        lanes = slice(quarter * LANES, (quarter + 1) * LANES)
        degrees[:512, lanes] = received[:, quarter * 16 : (quarter + 1) * 16, :].reshape(512, LANES)
    tail = jnp.sum(received[...].astype(F32)[:, 64:72, :], axis=0)
    extra = jnp.concatenate([tail[q : q + 1, :] for q in range(4)], axis=1)
    first = lax.broadcasted_iota(jnp.int32, (128, 512), 0) == 0
    degrees[512:640, :] = jnp.where(first, extra, 0.0).astype(BF16)
    for slot in range(2):
        for row in range(rows):
            total = jnp.dot(
                spread[slot, row * peers : (row + 1) * peers, :],
                degrees[...],
                preferred_element_type=F32,
            )
            for part in range(2):
                for half in range(2):
                    lane = (part * 2 + half) * LANES
                    block = total[:, lane : lane + LANES]
                    if weighted:
                        block = block * lat_w[row * peers : (row + 1) * peers, :]
                    wide[pl.ds(message_row(row, half, slot, part), peers, stride=24), :] = block
    out[...] = wide[...].reshape(out.shape).astype(BF16)


def degree_rows(wide, index, groups):
    parts = []
    for part in range(2):
        halves = [
            wide[pl.ds((part * 2 + half) * 16 + index, groups, stride=72), :] for half in range(2)
        ]
        parts.append(jnp.concatenate(halves, axis=1))
    return jnp.concatenate(parts, axis=0)


def extra_rows(wide, groups):
    parts = []
    for part in range(2):
        halves = [
            wide[pl.ds(64 + part * 2 + half, groups, stride=72), :] for half in range(2)
        ]
        parts.append(jnp.concatenate(halves, axis=1))
    return jnp.concatenate(parts, axis=0)


def store_rows(wide, start_of, values, groups):
    for part in range(2):
        for half in range(2):
            wide[pl.ds(start_of(part * 2 + half), groups, stride=72), :] = values[
                part * groups : (part + 1) * groups, half * LANES : (half + 1) * LANES
            ]


def pair_masks(lowest, degree):
    partner = 511 - degree
    return (
        lowest >= 0,
        degree >= lowest,
        partner >= lowest,
        511 - lowest == degree,
        511 - lowest == partner,
    )


def lowest_waves(own, first, shape):
    column = lax.broadcasted_iota(jnp.int32, first.shape, 1) == own[0]
    lowest = jnp.sum(jnp.where(column, first[...], 0), axis=1, keepdims=True)
    return jnp.broadcast_to(jnp.concatenate([lowest, lowest], axis=0), shape)


def filter_kernel(own, blocks, received, weight, first, out, wide, result):
    groups = received.shape[0]
    wide[...] = received[...].astype(F32).reshape(wide.shape)
    result[...] = jnp.zeros_like(result)
    extra = extra_rows(wide, groups)
    lowest = lowest_waves(own, first, extra.shape)
    extra_sum = jnp.zeros_like(extra)
    for index in range(8):
        mirror = 15 - index
        degree = blocks[2 * own[1]] * 8 + index
        _, near, far, extra_near, extra_far = pair_masks(lowest, degree)
        one = degree_rows(wide, index, groups)
        two = degree_rows(wide, mirror, groups)
        stacked = jnp.concatenate([one, two, extra], axis=0).astype(BF16)
        by_one = jnp.dot(stacked, weight[index], preferred_element_type=F32)
        by_two = jnp.dot(stacked, weight[mirror], preferred_element_type=F32)
        side = 2 * groups
        store_rows(
            wide=result,
            start_of=lambda quarter: quarter * 16 + index,
            values=jnp.where(near, by_one[:side], by_two[:side]),
            groups=groups,
        )
        store_rows(
            wide=result,
            start_of=lambda quarter: quarter * 16 + mirror,
            values=jnp.where(far, by_two[side : 2 * side], by_one[side : 2 * side]),
            groups=groups,
        )
        extra_sum = (
            extra_sum
            + jnp.where(extra_near, by_one[2 * side :], 0.0)
            + jnp.where(extra_far, by_two[2 * side :], 0.0)
        )
    store_rows(result, lambda quarter: 64 + quarter, extra_sum, groups)
    out[...] = result[...].reshape(out.shape).astype(BF16)


def filter_back_kernel(
    own, blocks, received, weight, first, coeffs, out, grad_w, wide, result, wide_coeffs
):
    groups = received.shape[0]
    wide[...] = received[...].astype(F32).reshape(wide.shape)
    wide_coeffs[...] = coeffs[...].astype(F32).reshape(wide.shape)
    result[...] = jnp.zeros_like(result)
    extra = extra_rows(wide, groups)
    lowest = lowest_waves(own, first, extra.shape)
    extra_sum = jnp.zeros_like(extra)
    kept_extra = extra_rows(wide_coeffs, groups)
    turned = (((1,), (1,)), ((), ()))
    summed = (((0,), (0,)), ((), ()))
    for index in range(8):
        mirror = 15 - index
        degree = blocks[2 * own[1]] * 8 + index
        _, near, far, extra_near, extra_far = pair_masks(lowest, degree)
        one = degree_rows(wide, index, groups)
        two = degree_rows(wide, mirror, groups)
        stacked = jnp.concatenate([one, two, extra], axis=0).astype(BF16)
        kept_one = degree_rows(wide_coeffs, index, groups)
        kept_two = degree_rows(wide_coeffs, mirror, groups)
        kept_near = jnp.concatenate(
            [
                jnp.where(near, kept_one, 0.0),
                jnp.where(far, 0.0, kept_two),
                jnp.where(extra_near, kept_extra, 0.0),
            ],
            axis=0,
        ).astype(BF16)
        kept_far = jnp.concatenate(
            [
                jnp.where(near, 0.0, kept_one),
                jnp.where(far, kept_two, 0.0),
                jnp.where(extra_far, kept_extra, 0.0),
            ],
            axis=0,
        ).astype(BF16)
        for place, kept in ((index, kept_near), (mirror, kept_far)):
            grad_w[place] = lax.dot_general(
                kept, stacked, summed, preferred_element_type=F32
            ).astype(BF16)
        by_one = lax.dot_general(stacked, weight[index], turned, preferred_element_type=F32)
        by_two = lax.dot_general(stacked, weight[mirror], turned, preferred_element_type=F32)
        side = 2 * groups
        store_rows(
            wide=result,
            start_of=lambda quarter: quarter * 16 + index,
            values=jnp.where(near, by_one[:side], by_two[:side]),
            groups=groups,
        )
        store_rows(
            wide=result,
            start_of=lambda quarter: quarter * 16 + mirror,
            values=jnp.where(far, by_two[side : 2 * side], by_one[side : 2 * side]),
            groups=groups,
        )
        extra_sum = (
            extra_sum
            + jnp.where(extra_near, by_one[2 * side :], 0.0)
            + jnp.where(extra_far, by_two[2 * side :], 0.0)
        )
    store_rows(result, lambda quarter: 64 + quarter, extra_sum, groups)
    out[...] = result[...].reshape(out.shape).astype(BF16)


def idft_row(table_back, wide, zero_at, row, peers, linear):
    pieces = []
    for slot in range(2):
        for part in range(2):
            halves = []
            for half in range(2):
                block = wide[pl.ds(message_row(row, half, slot, part), peers, stride=24), :]
                if zero_at is not None:
                    block = block * doubling(zero_at, slot, peers)
                halves.append(block.astype(BF16))
            pieces.append(jnp.concatenate(halves, axis=1))
    spectrum = jnp.concatenate(pieces, axis=0)
    linear[...] = jnp.dot(table_back[...], spectrum, preferred_element_type=F32)


def middle_kernel(own, received, table_back, grid_far, *refs):
    across, rows, lon, _ = grid_far.shape
    cot_far, spectrum, out_far = refs[:across], refs[across], refs[across + 1]
    wide, table, grid, cotangent, output, stages, linears = refs[across + 2 : across + 9]
    grid_in, cot_in, leaving = refs[across + 9 :]
    others = [pltpu.make_async_copy(grid_far, grid, grid_in)] + [
        pltpu.make_async_copy(cot_far[k], cotangent.at[own[0] ^ k], cot_in.at[k])
        for k in range(across)
    ]
    for copy in others:
        copy.start()
    zero_at = own[2]
    peers = received.shape[0]
    wide[...] = received[...].astype(F32).reshape(wide.shape)
    for row in range(rows):
        clear_pads(stages.at[row], across, lon)
        idft_row(table_back, wide, zero_at, row, peers, linears.at[row])
    table[...] = table_back[...].T
    for copy in others:
        copy.wait()
    leave = [
        pltpu.make_async_copy(output.at[row], out_far.at[:, row], leaving.at[row])
        for row in range(rows)
    ]
    for row in range(rows):
        linear, stage = linears.at[row], stages.at[row]
        for j in range(across):
            place = slice(j * ROW_PAD, j * ROW_PAD + lon)
            value = linear[place, :].astype(BF16).astype(F32)
            square = value * value
            bend = jnp.tanh(value * (GELU_A + (GELU_A * GELU_B) * square))
            gate = 0.5 + 0.5 * bend
            output[row, j] = (grid[j, row].astype(F32) + value * gate).astype(BF16)
            steep = value * (2.0 * GELU_A + (6.0 * GELU_A * GELU_B) * square)
            slope = gate + steep * (gate - gate * gate)
            stage[place, :] = (cotangent[j, row].astype(F32) * slope).astype(BF16)
        leave[row].start()
        dft_row(table, stage, zero_at, wide, row, peers)
    spectrum[...] = wide[...].reshape(spectrum.shape).astype(BF16)
    for copy in leave:
        copy.wait()


def last_kernel(own, received, table_back, *refs):
    across = len(refs) - 7
    cot_far, out_far = refs[:across], refs[across]
    wide, cotangent, output, linears, cot_in, leaving = refs[across + 1 :]
    _, rows, lon, _ = out_far.shape
    others = [
        pltpu.make_async_copy(cot_far[k], cotangent.at[own[0] ^ k], cot_in.at[k])
        for k in range(across)
    ]
    for copy in others:
        copy.start()
    peers = received.shape[0]
    wide[...] = received[...].astype(F32).reshape(wide.shape)
    leave = [
        pltpu.make_async_copy(output.at[row], out_far.at[:, row], leaving.at[row])
        for row in range(rows)
    ]
    for row in range(rows):
        linear = linears.at[row]
        idft_row(table_back, wide, None, row, peers, linear)
        if row == 0:
            for copy in others:
                copy.wait()
        for j in range(across):
            value = linear[j * ROW_PAD : j * ROW_PAD + lon, :].astype(BF16).astype(F32)
            output[row, j] = (cotangent[j, row].astype(F32) + value).astype(BF16)
        leave[row].start()
    for copy in leave:
        copy.wait()


def split_kernel(grid, *refs):
    lon, lat, _ = grid.shape
    wide = refs[-1]
    wide[...] = grid[...].astype(F32).reshape(wide.shape)
    across, rows = refs[0].shape[:2]
    for j in range(across):
        for row in range(rows):
            refs[0][j, row] = wide[pl.ds(row * across + j, lon, stride=lat), :].astype(BF16)


def split_far_kernel(own, grid, *refs):
    lon, lat, channels = grid.shape
    across = len(refs) - 3
    outs, (wide, bands, leaving) = refs[:across], refs[across:]
    rows = outs[0].shape[0]
    for lane in range(0, channels, LANES):
        lanes = slice(lane, lane + LANES)
        wide[...] = grid[:, :, lanes].astype(F32).reshape(wide.shape)
        for k in range(across):
            for row in range(rows):
                start = row * across + (own[0] ^ k)
                bands[k, row, :, lanes] = wide[pl.ds(start, lon, stride=lat), :].astype(BF16)
    copies = [
        pltpu.make_async_copy(bands.at[k], outs[k], leaving.at[k]) for k in range(across)
    ]
    for copy in copies:
        copy.start()
    for copy in copies:
        copy.wait()


def join_kernel(own, *refs):
    bands, out, wide = refs[:-2], refs[-2], refs[-1]
    lon, lat, _ = out.shape
    across, rows = len(bands), bands[0].shape[0]
    for k in range(across):
        for row in range(rows):
            start = row * across + (own[0] ^ k)
            wide[pl.ds(start, lon, stride=lat), :] = bands[k][row].astype(F32)
    out[...] = wide[...].reshape(out.shape).astype(BF16)


def degree_tables_kernel(own, blocks, waves, legendre, folded, spread, ordered, chosen):
    slots, lat_all, degree_count = legendre.shape
    count = degree_count // 16
    own_waves = [waves[own[3] * slots + slot] for slot in range(slots)]
    step = lax.broadcasted_iota(jnp.int32, (8, degree_count), 0)
    lane = lax.broadcasted_iota(jnp.int32, (8, degree_count), 1)
    chosen[...] = jnp.zeros_like(chosen)
    for pair in range(count):
        for slot in range(slots):
            pieces = []
            for block in (2 * pair, 2 * pair + 1):
                degree = blocks[block] * 8 + step
                if slot:
                    degree = jnp.where(
                        degree == own_waves[0], degree_count, degree_count - 1 - degree
                    )
                pieces.append(jnp.where(degree == lane, 1.0, 0.0))
            chosen[slot, pair * 16 : (pair + 1) * 16, :] = jnp.concatenate(pieces, axis=0).astype(
                BF16
            )
    sixteen = lax.broadcasted_iota(jnp.int32, (16, degree_count), 0)
    lanes = lax.broadcasted_iota(jnp.int32, (16, degree_count), 1)
    last = jnp.where(jnp.logical_and(sixteen == 0, lanes == own_waves[1]), 1.0, 0.0)
    chosen[1, degree_count : degree_count + 16, :] = last.astype(BF16)
    turned = (((1,), (1,)), ((), ()))
    for slot in range(slots):
        plane = legendre[slot].astype(F32).reshape(-1, lat_all // 256, 8, degree_count)
        for row in range(lat_all // 256):
            ordered[row * 256 : (row + 1) * 256, :] = (
                plane[:, row].reshape(256, degree_count).astype(BF16)
            )
        spread[slot] = lax.dot_general(
            ordered[...], chosen[slot], turned, preferred_element_type=F32
        ).astype(BF16)
        folded[:, slot * lat_all : (slot + 1) * lat_all] = lax.dot_general(
            chosen[slot, : folded.shape[0], :], ordered[...], turned, preferred_element_type=F32
        ).astype(BF16)


def tables(waves, lon_count, across):
    block = lon_count // across
    place = jnp.arange(ROW_PAD, dtype=jnp.int32)[:, None]
    angle = (2.0 * math.pi / lon_count) * (place * waves[None, :] % lon_count).astype(F32)
    size = jnp.where(place < block, 1.0 / math.sqrt(lon_count), 0.0)
    cosine, sine = jnp.cos(angle) * size, jnp.sin(angle) * size
    turn = jnp.arange(across, dtype=jnp.int32)[:, None] * waves[None, :] % across
    turn = (2.0 * math.pi / across) * turn.astype(F32)
    turn_cos, turn_sin = jnp.cos(turn)[:, None, :], jnp.sin(turn)[:, None, :]
    real = (cosine * turn_cos - sine * turn_sin).astype(BF16)
    imag = -(sine * turn_cos + cosine * turn_sin).astype(BF16)
    half = waves.shape[0] // 2
    back = jnp.concatenate(
        [real[..., :half], imag[..., :half], real[..., half:], imag[..., half:]], axis=-1
    )
    return back.reshape(across * ROW_PAD, 2 * waves.shape[0])


def body(field, cotangent, legendre, lat_weight, filter_weight, wave_order, deg_order):
    polar_count = lax.axis_size("polar")
    across = lax.axis_size("azimuth")
    peers = polar_count * across
    both = ("polar", "azimuth")
    lat_rows, lon_cols, channels = field.shape
    rows = lat_rows // across
    slots, lat_all, degree_count = legendre.shape
    block_size = degree_count // deg_order.shape[0]
    polar, azimuth = lax.axis_index("polar"), lax.axis_index("azimuth")
    device = polar * across + azimuth
    lon_count = lon_cols * across

    vmem = pl.BlockSpec(memory_space=pltpu.VMEM)
    smem = pl.BlockSpec(memory_space=pltpu.SMEM)
    far = pl.BlockSpec(memory_space=pltpu.HBM)
    pairs = wave_order.reshape(peers, slots)
    waves = pairs.T.reshape(-1)
    zero_at = jnp.sum(jnp.where(waves == 0, jnp.arange(waves.shape[0], dtype=jnp.int32), 0))
    own = jnp.stack([azimuth, polar, zero_at, device])
    band = (rows, lon_cols, channels)
    bands_shape = (across, *band)
    one_band = jax.ShapeDtypeStruct(band, BF16)
    trade = [[(i, i ^ k) for i in range(across)] for k in range(across)]

    def kernel_call(kernel, outs, in_specs, out_specs, scratch, mib, cost, *operands):
        return pl.pallas_call(
            kernel,
            out_shape=outs,
            in_specs=in_specs,
            out_specs=out_specs,
            scratch_shapes=scratch,
            compiler_params=pltpu.CompilerParams(vmem_limit_bytes=mib * MIB),
            cost_estimate=pl.CostEstimate(
                flops=cost, bytes_accessed=cost // 1000, transcendentals=0
            ),
        )(*operands)

    def half_bands(kernel, ins, outs, scalars, *operands):
        def spec(array):
            inner = tuple(array.shape[:-1])
            return pl.BlockSpec((*inner, LANES), lambda h: (0,) * len(inner) + (h,))

        return pl.pallas_call(
            kernel,
            grid=(channels // LANES,),
            out_shape=outs,
            in_specs=[smem] * len(scalars) + [spec(x) for x in ins],
            out_specs=jax.tree.map(spec, outs),
            scratch_shapes=[pltpu.VMEM((lon_cols * lat_rows, LANES), F32)],
            compiler_params=pltpu.CompilerParams(vmem_limit_bytes=56 * MIB),
            cost_estimate=pl.CostEstimate(flops=2_000, bytes_accessed=2_000, transcendentals=0),
        )(*scalars, *operands)

    def join_bands(bands):
        out = jax.ShapeDtypeStruct((lon_cols, lat_rows, channels), BF16)
        return jnp.transpose(half_bands(join_kernel, bands, out, [own], *bands), (1, 0, 2))

    def piece(bands, k):
        if isinstance(bands, (list, tuple)):
            return bands[k]
        return lax.dynamic_index_in_dim(bands, azimuth ^ k, 0, keepdims=False)

    def beside(payload, axes, bands, kinds, done):
        payload, bands = lax.optimization_barrier((payload, bands))
        moved = [lax.ppermute(piece(bands, k), "azimuth", trade[k]) for k in kinds]
        payload = exchange(payload, axes)
        payload, bands, moved = lax.optimization_barrier((payload, bands, moved))
        done.update(zip(kinds, moved))
        return payload, bands

    groups = ((2, 6, 4, 5), (1, 3, 7))

    turned_field = jnp.transpose(field, (1, 0, 2))
    grid = exchange(
        half_bands(
            split_kernel,
            [turned_field],
            jax.ShapeDtypeStruct(bands_shape, BF16),
            [],
            turned_field,
        ),
        "azimuth",
    )

    table_back = tables(waves, lon_count, across)
    folded, spread = kernel_call(
        degree_tables_kernel,
        (
            jax.ShapeDtypeStruct((degree_count + LANES // 2, slots * lat_all), BF16),
            jax.ShapeDtypeStruct((slots, lat_all, degree_count + LANES), BF16),
        ),
        [smem, smem, smem, vmem],
        (vmem, vmem),
        [
            pltpu.VMEM((lat_all, degree_count), BF16),
            pltpu.VMEM((slots, degree_count + LANES, degree_count), BF16),
        ],
        32,
        1000,
        own,
        deg_order,
        wave_order,
        legendre,
    )
    lat_w = jnp.broadcast_to(
        lat_weight.reshape(polar_count, rows, across).transpose(1, 0, 2).reshape(-1, 1),
        (lat_all, LANES),
    )
    first = pairs[:, 0].reshape(polar_count, across)
    cot_send = kernel_call(
        split_far_kernel,
        (one_band,) * across,
        [smem, vmem],
        (far,) * across,
        [
            pltpu.VMEM((lon_cols * lat_rows, LANES), F32),
            pltpu.VMEM(bands_shape, BF16),
            pltpu.SemaphoreType.DMA((across,)),
        ],
        24,
        1000,
        own,
        jnp.transpose(cotangent, (1, 0, 2)),
    )
    grid, table_back, folded, spread, lat_w, first, cot_send = lax.optimization_barrier(
        (grid, table_back, folded, spread, lat_w, first, cot_send)
    )

    message = (peers, 8 * rows, LANES)
    degree_message = (polar_count, 72, LANES)
    wide = pltpu.VMEM((peers * 8 * rows, LANES), F32)
    degree_wide = pltpu.VMEM((polar_count * 72, LANES), F32)
    stages = pltpu.VMEM((rows, across * ROW_PAD, channels), BF16)
    linears = pltpu.VMEM((rows, across * ROW_PAD, channels), F32)
    held_bands = pltpu.VMEM(bands_shape, BF16)
    held_rows = pltpu.VMEM((rows, across, lon_cols, channels), BF16)
    sems = pltpu.SemaphoreType.DMA
    held_table = pltpu.VMEM(table_back.shape[::-1], BF16)
    spectrum_shape = jax.ShapeDtypeStruct(message, BF16)
    degree_shape = jax.ShapeDtypeStruct(degree_message, BF16)
    local_degrees = filter_weight.shape[0]

    def analysis(received, weighted):
        return kernel_call(
            functools.partial(analysis_kernel, weighted),
            degree_shape,
            [vmem, vmem, far],
            vmem,
            [
                wide,
                pltpu.VMEM((slots * lat_all, 4 * LANES), BF16),
                pltpu.VMEM(folded.shape, BF16),
                sems((PIECES,)),
            ],
            APART,
            800_000_000,
            received,
            lat_w,
            folded,
        )

    def synthesis(received, weighted):
        return kernel_call(
            functools.partial(synthesis_kernel, weighted),
            spectrum_shape,
            [vmem] * 3,
            vmem,
            [wide, pltpu.VMEM((degree_count + LANES, 4 * LANES), BF16)],
            24,
            800_000_000,
            received,
            lat_w,
            spread,
        )

    spectrum = kernel_call(
        dft_kernel,
        spectrum_shape,
        [vmem, vmem],
        vmem,
        [wide, held_table, stages],
        24,
        2_400_000_000,
        grid,
        table_back,
    )
    cot_bands = {0: cot_send[0]}
    arrived, cot_send = beside(spectrum, both, cot_send, groups[0], cot_bands)
    coeffs = analysis(arrived, True)
    coeffs, cot_send = beside(coeffs, "polar", cot_send, groups[1], cot_bands)
    filtered = kernel_call(
        filter_kernel,
        degree_shape,
        [smem, smem, vmem, vmem, vmem],
        vmem,
        [degree_wide, degree_wide],
        24,
        300_000_000,
        own,
        deg_order,
        coeffs,
        filter_weight,
        first,
    )
    filtered = exchange(filtered, "polar")
    cot_bands = [cot_bands[k] for k in range(across)]
    arrived = exchange(synthesis(filtered, False), both)
    grad_spec, output_bands = kernel_call(
        middle_kernel,
        (spectrum_shape, jax.ShapeDtypeStruct(bands_shape, BF16)),
        [smem, vmem, vmem] + [far] * (1 + across),
        (vmem, far),
        [
            wide,
            held_table,
            held_bands,
            held_bands,
            held_rows,
            stages,
            linears,
            sems,
            sems((across,)),
            sems((rows,)),
        ],
        WHOLE,
        4_800_000_000,
        own,
        arrived,
        table_back,
        grid,
        *cot_bands,
    )
    output_moved = {}
    arrived, output_bands = beside(grad_spec, both, output_bands, groups[0], output_moved)
    grad_filtered = analysis(arrived, False)
    grad_filtered, output_bands = beside(
        grad_filtered, "polar", output_bands, groups[1], output_moved
    )
    grad_coeffs, weight_terms = kernel_call(
        filter_back_kernel,
        (degree_shape, jax.ShapeDtypeStruct(filter_weight.shape, BF16)),
        [smem, smem, vmem, vmem, vmem, vmem],
        (vmem, vmem),
        [degree_wide, degree_wide, degree_wide],
        24,
        600_000_000,
        own,
        deg_order,
        grad_filtered,
        filter_weight,
        first,
        coeffs,
    )
    grad_coeffs = exchange(grad_coeffs, "polar")
    output_moved[0] = piece(output_bands, 0)
    grad_weight = lax.psum_scatter(
        weight_terms, "azimuth", scatter_dimension=1, tiled=True
    ).astype(F32)
    arrived = exchange(synthesis(grad_coeffs, True), both)
    grad_bands = kernel_call(
        last_kernel,
        jax.ShapeDtypeStruct(bands_shape, BF16),
        [smem, vmem, vmem] + [far] * across,
        far,
        [wide, held_bands, held_rows, linears, sems((across,)), sems((rows,))],
        WHOLE,
        2_400_000_000,
        own,
        arrived,
        table_back,
        *cot_bands,
    )
    output_moved = [output_moved[k] for k in range(across)]
    grad_bands, output_moved = lax.optimization_barrier((grad_bands, output_moved))
    output = join_bands(output_moved)
    grad_field = (
        exchange(grad_bands, "azimuth")
        .transpose(1, 0, 2, 3)
        .reshape(lat_rows, lon_cols, channels)
    )
    return (output, grad_field, grad_weight)


def solution(mesh):
    placed = (
        P("polar", "azimuth", None),
        P("polar", "azimuth", None),
        P(("polar", "azimuth"), None, None),
        P(),
        P("polar", None, None),
        P(),
        P(),
    )
    return jax.shard_map(
        body,
        mesh=mesh,
        in_specs=placed,
        out_specs=(
            P("polar", "azimuth", None),
            P("polar", "azimuth", None),
            P("polar", "azimuth", None),
        ),
        check_vma=False,
    )
```

```python
import functools
import math

import jax
import jax.numpy as jnp
from jax import lax
from jax.experimental import pallas as pl
from jax.experimental.pallas import tpu as pltpu
from jax.sharding import PartitionSpec as P

BF16 = jnp.bfloat16
F32 = jnp.float32
LANES = 128
ROW_PAD = 192
MIB = 1024 * 1024
WHOLE = 56
LAST = 52
APART = 56
PIECES = 4
GELU_A = math.sqrt(2.0 / math.pi)
GELU_B = 0.044715


def exchange(payload, axes):
    return lax.all_to_all(payload, axes, split_axis=0, concat_axis=0, tiled=True)


def message_row(row, half, slot, part):
    return row * 8 + half * 4 + slot * 2 + part


def unpack_rows(received, wide, row, slot, part, peers):
    halves = [
        wide[pl.ds(message_row(row, half, slot, part), peers, stride=24), :] for half in range(2)
    ]
    return jnp.concatenate(halves, axis=1)


def doubling(zero_at, slot, peers):
    place = slot * peers + lax.broadcasted_iota(jnp.int32, (peers, LANES), 0)
    return jnp.where(place == zero_at, 1.0, 2.0)


def clear_pads(stage, across, lon):
    start = lon // 16 * 16
    for j in range(across):
        stage[j * ROW_PAD + start : (j + 1) * ROW_PAD, :] = jnp.zeros(
            (ROW_PAD - start, stage.shape[1]), BF16
        )


def dft_row(table, grid_rows, zero_at, wide, row, peers):
    total = jnp.dot(table[...], grid_rows[...], preferred_element_type=F32)
    for slot in range(2):
        for part in range(2):
            start = (slot * 2 + part) * peers
            for half in range(2):
                block = total[start : start + peers, half * LANES : (half + 1) * LANES]
                if zero_at is not None:
                    block = block * doubling(zero_at, slot, peers)
                wide[pl.ds(message_row(row, half, slot, part), peers, stride=24), :] = block


def dft_kernel(grid, table_back, out, wide, table, stages):
    across, rows, lon, _ = grid.shape
    peers = out.shape[0]
    table[...] = table_back[...].T
    for row in range(rows):
        stage = stages.at[row]
        clear_pads(stage, across, lon)
        for j in range(across):
            stage[j * ROW_PAD : j * ROW_PAD + lon, :] = grid[j, row]
        dft_row(table, stage, None, wide, row, peers)
    out[...] = wide[...].reshape(out.shape).astype(BF16)


def analysis_kernel(weighted, received, lat_w, folded_far, out, wide, columns, folded, arrival):
    size = folded.shape[0] // PIECES
    fetches = [
        pltpu.make_async_copy(
            folded_far.at[pl.ds(c * size, size)], folded.at[pl.ds(c * size, size)], arrival.at[c]
        )
        for c in range(PIECES)
    ]
    for fetch in fetches:
        fetch.start()
    peers = received.shape[0]
    wide[...] = received[...].astype(F32).reshape(wide.shape)
    rows = received.shape[1] // 8
    for slot in range(2):
        for row in range(rows):
            start = (slot * rows + row) * peers
            for part in range(2):
                for half in range(2):
                    block = wide[
                        pl.ds(message_row(row, half, slot, part), peers, stride=24), :
                    ]
                    if weighted:
                        block = block * lat_w[row * peers : (row + 1) * peers, :]
                    lane = (part * 2 + half) * LANES
                    columns[start : start + peers, lane : lane + LANES] = block.astype(BF16)
    for fetch in fetches:
        fetch.wait()
    total = jnp.dot(folded[...], columns[...], preferred_element_type=F32).astype(BF16)
    groups = out.shape[0]
    for quarter in range(4):
        lanes = slice(quarter * LANES, (quarter + 1) * LANES)
        out[:, quarter * 16 : (quarter + 1) * 16, :] = total[:512, lanes].reshape(groups, 16, LANES)
    extra = total[512:528, :].astype(F32)
    tail = jnp.concatenate(
        [extra[0:1, q * LANES : (q + 1) * LANES] for q in range(4)]
        + [jnp.zeros((4, LANES), F32)],
        axis=0,
    )
    out[:, 64:72, :] = jnp.broadcast_to(tail.astype(BF16)[None], (groups, 8, LANES))


def synthesis_kernel(weighted, received, lat_w, spread, out, wide, degrees):
    peers = out.shape[0]
    groups = received.shape[0]
    rows = out.shape[1] // 8
    for quarter in range(4):
        lanes = slice(quarter * LANES, (quarter + 1) * LANES)
        degrees[:512, lanes] = received[:, quarter * 16 : (quarter + 1) * 16, :].reshape(512, LANES)
    tail = jnp.sum(received[...].astype(F32)[:, 64:72, :], axis=0)
    extra = jnp.concatenate([tail[q : q + 1, :] for q in range(4)], axis=1)
    first = lax.broadcasted_iota(jnp.int32, (128, 512), 0) == 0
    degrees[512:640, :] = jnp.where(first, extra, 0.0).astype(BF16)
    for slot in range(2):
        for row in range(rows):
            total = jnp.dot(
                spread[slot, row * peers : (row + 1) * peers, :],
                degrees[...],
                preferred_element_type=F32,
            )
            for part in range(2):
                for half in range(2):
                    lane = (part * 2 + half) * LANES
                    block = total[:, lane : lane + LANES]
                    if weighted:
                        block = block * lat_w[row * peers : (row + 1) * peers, :]
                    wide[pl.ds(message_row(row, half, slot, part), peers, stride=24), :] = block
    out[...] = wide[...].reshape(out.shape).astype(BF16)


def degree_rows(wide, index, groups):
    parts = []
    for part in range(2):
        halves = [
            wide[pl.ds((part * 2 + half) * 16 + index, groups, stride=72), :] for half in range(2)
        ]
        parts.append(jnp.concatenate(halves, axis=1))
    return jnp.concatenate(parts, axis=0)


def extra_rows(wide, groups):
    parts = []
    for part in range(2):
        halves = [
            wide[pl.ds(64 + part * 2 + half, groups, stride=72), :] for half in range(2)
        ]
        parts.append(jnp.concatenate(halves, axis=1))
    return jnp.concatenate(parts, axis=0)


def store_rows(wide, start_of, values, groups):
    for part in range(2):
        for half in range(2):
            wide[pl.ds(start_of(part * 2 + half), groups, stride=72), :] = values[
                part * groups : (part + 1) * groups, half * LANES : (half + 1) * LANES
            ]


def pair_masks(lowest, degree):
    partner = 511 - degree
    return (
        lowest >= 0,
        degree >= lowest,
        partner >= lowest,
        511 - lowest == degree,
        511 - lowest == partner,
    )


def lowest_waves(own, first, shape):
    column = lax.broadcasted_iota(jnp.int32, first.shape, 1) == own[0]
    lowest = jnp.sum(jnp.where(column, first[...], 0), axis=1, keepdims=True)
    return jnp.broadcast_to(jnp.concatenate([lowest, lowest], axis=0), shape)


def filter_kernel(contracted, own, blocks, received, weight, first, out, wide, result):
    groups = received.shape[0]
    dims = (((1,), (contracted,)), ((), ()))
    wide[...] = received[...].astype(F32).reshape(wide.shape)
    result[...] = jnp.zeros_like(result)
    extra = extra_rows(wide, groups)
    lowest = lowest_waves(own, first, extra.shape)
    extra_sum = jnp.zeros_like(extra)
    for index in range(8):
        mirror = 15 - index
        degree = blocks[2 * own[1]] * 8 + index
        _, near, far, extra_near, extra_far = pair_masks(lowest, degree)
        one = degree_rows(wide, index, groups)
        two = degree_rows(wide, mirror, groups)
        stacked = jnp.concatenate([one, two, extra], axis=0).astype(BF16)
        by_one = lax.dot_general(stacked, weight[index], dims, preferred_element_type=F32)
        by_two = lax.dot_general(stacked, weight[mirror], dims, preferred_element_type=F32)
        side = 2 * groups
        store_rows(
            wide=result,
            start_of=lambda quarter: quarter * 16 + index,
            values=jnp.where(near, by_one[:side], by_two[:side]),
            groups=groups,
        )
        store_rows(
            wide=result,
            start_of=lambda quarter: quarter * 16 + mirror,
            values=jnp.where(far, by_two[side : 2 * side], by_one[side : 2 * side]),
            groups=groups,
        )
        extra_sum = (
            extra_sum
            + jnp.where(extra_near, by_one[2 * side :], 0.0)
            + jnp.where(extra_far, by_two[2 * side :], 0.0)
        )
    store_rows(result, lambda quarter: 64 + quarter, extra_sum, groups)
    out[...] = result[...].reshape(out.shape).astype(BF16)


def weight_kernel(own, blocks, received, coeffs, first, grad_w, wide, wide_coeffs):
    groups = received.shape[0]
    wide[...] = received[...].astype(F32).reshape(wide.shape)
    wide_coeffs[...] = coeffs[...].astype(F32).reshape(wide.shape)
    extra = extra_rows(wide, groups)
    kept_extra = extra_rows(wide_coeffs, groups)
    lowest = lowest_waves(own, first, extra.shape)
    summed = (((0,), (0,)), ((), ()))
    for index in range(8):
        mirror = 15 - index
        degree = blocks[2 * own[1]] * 8 + index
        _, near, far, extra_near, extra_far = pair_masks(lowest, degree)
        one = degree_rows(wide, index, groups)
        two = degree_rows(wide, mirror, groups)
        stacked = jnp.concatenate([one, two, extra], axis=0).astype(BF16)
        kept_one = degree_rows(wide_coeffs, index, groups)
        kept_two = degree_rows(wide_coeffs, mirror, groups)
        kept_near = jnp.concatenate(
            [
                jnp.where(near, kept_one, 0.0),
                jnp.where(far, 0.0, kept_two),
                jnp.where(extra_near, kept_extra, 0.0),
            ],
            axis=0,
        ).astype(BF16)
        kept_far = jnp.concatenate(
            [
                jnp.where(near, 0.0, kept_one),
                jnp.where(far, kept_two, 0.0),
                jnp.where(extra_far, kept_extra, 0.0),
            ],
            axis=0,
        ).astype(BF16)
        for place, kept in ((index, kept_near), (mirror, kept_far)):
            grad_w[place] = lax.dot_general(
                kept, stacked, summed, preferred_element_type=F32
            ).astype(BF16)


def idft_row(table_back, wide, zero_at, row, peers, linear):
    pieces = []
    for slot in range(2):
        for part in range(2):
            halves = []
            for half in range(2):
                block = wide[pl.ds(message_row(row, half, slot, part), peers, stride=24), :]
                if zero_at is not None:
                    block = block * doubling(zero_at, slot, peers)
                halves.append(block.astype(BF16))
            pieces.append(jnp.concatenate(halves, axis=1))
    spectrum = jnp.concatenate(pieces, axis=0)
    linear[...] = jnp.dot(table_back[...], spectrum, preferred_element_type=F32)


def middle_kernel(own, received, table_back, grid_far, *refs):
    across, rows, lon, _ = grid_far.shape
    cot_far, spectrum, out_far = refs[:across], refs[across], refs[across + 1]
    wide, table, grid, cotangent, output, stages, linears = refs[across + 2 : across + 9]
    grid_in, cot_in, leaving = refs[across + 9 :]
    others = [pltpu.make_async_copy(grid_far, grid, grid_in)] + [
        pltpu.make_async_copy(cot_far[k], cotangent.at[own[0] ^ k], cot_in.at[k])
        for k in range(across)
    ]
    for copy in others:
        copy.start()
    zero_at = own[2]
    peers = received.shape[0]
    wide[...] = received[...].astype(F32).reshape(wide.shape)
    for row in range(rows):
        clear_pads(stages.at[row], across, lon)
        idft_row(table_back, wide, zero_at, row, peers, linears.at[row])
    table[...] = table_back[...].T
    for copy in others:
        copy.wait()
    leave = [
        pltpu.make_async_copy(output.at[row], out_far.at[:, row], leaving.at[row])
        for row in range(rows)
    ]
    for row in range(rows):
        linear, stage = linears.at[row], stages.at[row]
        for j in range(across):
            place = slice(j * ROW_PAD, j * ROW_PAD + lon)
            value = linear[place, :].astype(BF16).astype(F32)
            square = value * value
            bend = jnp.tanh(value * (GELU_A + (GELU_A * GELU_B) * square))
            gate = 0.5 + 0.5 * bend
            output[row, j] = (grid[j, row].astype(F32) + value * gate).astype(BF16)
            steep = value * (2.0 * GELU_A + (6.0 * GELU_A * GELU_B) * square)
            slope = gate + steep * (gate - gate * gate)
            stage[place, :] = (cotangent[j, row].astype(F32) * slope).astype(BF16)
        leave[row].start()
        dft_row(table, stage, zero_at, wide, row, peers)
    spectrum[...] = wide[...].reshape(spectrum.shape).astype(BF16)
    for copy in leave:
        copy.wait()


def last_kernel(own, received, table_back, *refs):
    across = len(refs) - 7
    cot_far, out_far = refs[:across], refs[across]
    wide, cotangent, output, linears, cot_in, leaving = refs[across + 1 :]
    _, rows, lon, _ = out_far.shape
    others = [
        pltpu.make_async_copy(cot_far[k], cotangent.at[own[0] ^ k], cot_in.at[k])
        for k in range(across)
    ]
    for copy in others:
        copy.start()
    peers = received.shape[0]
    wide[...] = received[...].astype(F32).reshape(wide.shape)
    leave = [
        pltpu.make_async_copy(output.at[row], out_far.at[:, row], leaving.at[row])
        for row in range(rows)
    ]
    for row in range(rows):
        linear = linears.at[row]
        idft_row(table_back, wide, None, row, peers, linear)
        if row == 0:
            for copy in others:
                copy.wait()
        for j in range(across):
            value = linear[j * ROW_PAD : j * ROW_PAD + lon, :].astype(BF16).astype(F32)
            output[row, j] = (cotangent[j, row].astype(F32) + value).astype(BF16)
        leave[row].start()
    for copy in leave:
        copy.wait()


def split_kernel(grid, *refs):
    lon, lat, _ = grid.shape
    wide = refs[-1]
    wide[...] = grid[...].astype(F32).reshape(wide.shape)
    across, rows = refs[0].shape[:2]
    for j in range(across):
        for row in range(rows):
            refs[0][j, row] = wide[pl.ds(row * across + j, lon, stride=lat), :].astype(BF16)


def split_far_kernel(own, grid, *refs):
    lon, lat, channels = grid.shape
    across = len(refs) - 3
    outs, (wide, bands, leaving) = refs[:across], refs[across:]
    rows = outs[0].shape[0]
    for lane in range(0, channels, LANES):
        lanes = slice(lane, lane + LANES)
        wide[...] = grid[:, :, lanes].astype(F32).reshape(wide.shape)
        for k in range(across):
            for row in range(rows):
                start = row * across + (own[0] ^ k)
                bands[k, row, :, lanes] = wide[pl.ds(start, lon, stride=lat), :].astype(BF16)
    copies = [
        pltpu.make_async_copy(bands.at[k], outs[k], leaving.at[k]) for k in range(across)
    ]
    for copy in copies:
        copy.start()
    for copy in copies:
        copy.wait()


def join_kernel(own, *refs):
    bands, out, wide = refs[:-2], refs[-2], refs[-1]
    lon, lat, _ = out.shape
    across, rows = len(bands), bands[0].shape[0]
    for k in range(across):
        for row in range(rows):
            start = row * across + (own[0] ^ k)
            wide[pl.ds(start, lon, stride=lat), :] = bands[k][row].astype(F32)
    out[...] = wide[...].reshape(out.shape).astype(BF16)


def degree_tables_kernel(own, blocks, waves, legendre, folded, spread, ordered, chosen):
    slots, lat_all, degree_count = legendre.shape
    count = degree_count // 16
    own_waves = [waves[own[3] * slots + slot] for slot in range(slots)]
    step = lax.broadcasted_iota(jnp.int32, (8, degree_count), 0)
    lane = lax.broadcasted_iota(jnp.int32, (8, degree_count), 1)
    chosen[...] = jnp.zeros_like(chosen)
    for pair in range(count):
        for slot in range(slots):
            pieces = []
            for block in (2 * pair, 2 * pair + 1):
                degree = blocks[block] * 8 + step
                if slot:
                    degree = jnp.where(
                        degree == own_waves[0], degree_count, degree_count - 1 - degree
                    )
                pieces.append(jnp.where(degree == lane, 1.0, 0.0))
            chosen[slot, pair * 16 : (pair + 1) * 16, :] = jnp.concatenate(pieces, axis=0).astype(
                BF16
            )
    sixteen = lax.broadcasted_iota(jnp.int32, (16, degree_count), 0)
    lanes = lax.broadcasted_iota(jnp.int32, (16, degree_count), 1)
    last = jnp.where(jnp.logical_and(sixteen == 0, lanes == own_waves[1]), 1.0, 0.0)
    chosen[1, degree_count : degree_count + 16, :] = last.astype(BF16)
    turned = (((1,), (1,)), ((), ()))
    for slot in range(slots):
        plane = legendre[slot].astype(F32).reshape(-1, lat_all // 256, 8, degree_count)
        for row in range(lat_all // 256):
            ordered[row * 256 : (row + 1) * 256, :] = (
                plane[:, row].reshape(256, degree_count).astype(BF16)
            )
        spread[slot] = lax.dot_general(
            ordered[...], chosen[slot], turned, preferred_element_type=F32
        ).astype(BF16)
        folded[:, slot * lat_all : (slot + 1) * lat_all] = lax.dot_general(
            chosen[slot, : folded.shape[0], :], ordered[...], turned, preferred_element_type=F32
        ).astype(BF16)


def tables(waves, lon_count, across):
    block = lon_count // across
    place = jnp.arange(ROW_PAD, dtype=jnp.int32)[:, None]
    angle = (2.0 * math.pi / lon_count) * (place * waves[None, :] % lon_count).astype(F32)
    size = jnp.where(place < block, 1.0 / math.sqrt(lon_count), 0.0)
    cosine, sine = jnp.cos(angle) * size, jnp.sin(angle) * size
    turn = jnp.arange(across, dtype=jnp.int32)[:, None] * waves[None, :] % across
    turn = (2.0 * math.pi / across) * turn.astype(F32)
    turn_cos, turn_sin = jnp.cos(turn)[:, None, :], jnp.sin(turn)[:, None, :]
    real = (cosine * turn_cos - sine * turn_sin).astype(BF16)
    imag = -(sine * turn_cos + cosine * turn_sin).astype(BF16)
    half = waves.shape[0] // 2
    back = jnp.concatenate(
        [real[..., :half], imag[..., :half], real[..., half:], imag[..., half:]], axis=-1
    )
    return back.reshape(across * ROW_PAD, 2 * waves.shape[0])


def body(field, cotangent, legendre, lat_weight, filter_weight, wave_order, deg_order):
    polar_count = lax.axis_size("polar")
    across = lax.axis_size("azimuth")
    peers = polar_count * across
    both = ("polar", "azimuth")
    lat_rows, lon_cols, channels = field.shape
    rows = lat_rows // across
    slots, lat_all, degree_count = legendre.shape
    block_size = degree_count // deg_order.shape[0]
    polar, azimuth = lax.axis_index("polar"), lax.axis_index("azimuth")
    device = polar * across + azimuth
    lon_count = lon_cols * across

    vmem = pl.BlockSpec(memory_space=pltpu.VMEM)
    smem = pl.BlockSpec(memory_space=pltpu.SMEM)
    far = pl.BlockSpec(memory_space=pltpu.HBM)
    pairs = wave_order.reshape(peers, slots)
    waves = pairs.T.reshape(-1)
    zero_at = jnp.sum(jnp.where(waves == 0, jnp.arange(waves.shape[0], dtype=jnp.int32), 0))
    own = jnp.stack([azimuth, polar, zero_at, device])
    band = (rows, lon_cols, channels)
    bands_shape = (across, *band)
    one_band = jax.ShapeDtypeStruct(band, BF16)
    trade = [[(i, i ^ k) for i in range(across)] for k in range(across)]

    def kernel_call(kernel, outs, in_specs, out_specs, scratch, mib, cost, *operands):
        return pl.pallas_call(
            kernel,
            out_shape=outs,
            in_specs=in_specs,
            out_specs=out_specs,
            scratch_shapes=scratch,
            compiler_params=pltpu.CompilerParams(vmem_limit_bytes=mib * MIB),
            cost_estimate=pl.CostEstimate(
                flops=cost, bytes_accessed=cost // 1000, transcendentals=0
            ),
        )(*operands)

    def half_bands(kernel, ins, outs, scalars, *operands):
        def spec(array):
            inner = tuple(array.shape[:-1])
            return pl.BlockSpec((*inner, LANES), lambda h: (0,) * len(inner) + (h,))

        return pl.pallas_call(
            kernel,
            grid=(channels // LANES,),
            out_shape=outs,
            in_specs=[smem] * len(scalars) + [spec(x) for x in ins],
            out_specs=jax.tree.map(spec, outs),
            scratch_shapes=[pltpu.VMEM((lon_cols * lat_rows, LANES), F32)],
            compiler_params=pltpu.CompilerParams(vmem_limit_bytes=56 * MIB),
            cost_estimate=pl.CostEstimate(flops=2_000, bytes_accessed=2_000, transcendentals=0),
        )(*scalars, *operands)

    def join_bands(bands):
        out = jax.ShapeDtypeStruct((lon_cols, lat_rows, channels), BF16)
        return jnp.transpose(half_bands(join_kernel, bands, out, [own], *bands), (1, 0, 2))

    def piece(bands, k):
        if isinstance(bands, (list, tuple)):
            return bands[k]
        return lax.dynamic_index_in_dim(bands, azimuth ^ k, 0, keepdims=False)

    def beside(payload, axes, bands, kinds, done):
        payload, bands = lax.optimization_barrier((payload, bands))
        moved = [lax.ppermute(piece(bands, k), "azimuth", trade[k]) for k in kinds]
        payload = exchange(payload, axes)
        payload, bands, moved = lax.optimization_barrier((payload, bands, moved))
        done.update(zip(kinds, moved))
        return payload, bands

    groups = ((2, 6, 4, 5), (1, 3, 7))

    turned_field = jnp.transpose(field, (1, 0, 2))
    grid = exchange(
        half_bands(
            split_kernel,
            [turned_field],
            jax.ShapeDtypeStruct(bands_shape, BF16),
            [],
            turned_field,
        ),
        "azimuth",
    )

    table_back = tables(waves, lon_count, across)
    folded, spread = kernel_call(
        degree_tables_kernel,
        (
            jax.ShapeDtypeStruct((degree_count + LANES // 2, slots * lat_all), BF16),
            jax.ShapeDtypeStruct((slots, lat_all, degree_count + LANES), BF16),
        ),
        [smem, smem, smem, vmem],
        (vmem, vmem),
        [
            pltpu.VMEM((lat_all, degree_count), BF16),
            pltpu.VMEM((slots, degree_count + LANES, degree_count), BF16),
        ],
        32,
        1000,
        own,
        deg_order,
        wave_order,
        legendre,
    )
    lat_w = jnp.broadcast_to(
        lat_weight.reshape(polar_count, rows, across).transpose(1, 0, 2).reshape(-1, 1),
        (lat_all, LANES),
    )
    first = pairs[:, 0].reshape(polar_count, across)
    cot_send = kernel_call(
        split_far_kernel,
        (one_band,) * across,
        [smem, vmem],
        (far,) * across,
        [
            pltpu.VMEM((lon_cols * lat_rows, LANES), F32),
            pltpu.VMEM(bands_shape, BF16),
            pltpu.SemaphoreType.DMA((across,)),
        ],
        24,
        1000,
        own,
        jnp.transpose(cotangent, (1, 0, 2)),
    )
    grid, table_back, folded, spread, lat_w, first, cot_send = lax.optimization_barrier(
        (grid, table_back, folded, spread, lat_w, first, cot_send)
    )

    message = (peers, 8 * rows, LANES)
    degree_message = (polar_count, 72, LANES)
    wide = pltpu.VMEM((peers * 8 * rows, LANES), F32)
    degree_wide = pltpu.VMEM((polar_count * 72, LANES), F32)
    stages = pltpu.VMEM((rows, across * ROW_PAD, channels), BF16)
    linears = pltpu.VMEM((rows, across * ROW_PAD, channels), F32)
    held_bands = pltpu.VMEM(bands_shape, BF16)
    held_rows = pltpu.VMEM((rows, across, lon_cols, channels), BF16)
    sems = pltpu.SemaphoreType.DMA
    held_table = pltpu.VMEM(table_back.shape[::-1], BF16)
    spectrum_shape = jax.ShapeDtypeStruct(message, BF16)
    degree_shape = jax.ShapeDtypeStruct(degree_message, BF16)
    local_degrees = filter_weight.shape[0]

    def analysis(received, weighted):
        return kernel_call(
            functools.partial(analysis_kernel, weighted),
            degree_shape,
            [vmem, vmem, far],
            vmem,
            [
                wide,
                pltpu.VMEM((slots * lat_all, 4 * LANES), BF16),
                pltpu.VMEM(folded.shape, BF16),
                sems((PIECES,)),
            ],
            APART,
            800_000_000,
            received,
            lat_w,
            folded,
        )

    def synthesis(received, weighted):
        return kernel_call(
            functools.partial(synthesis_kernel, weighted),
            spectrum_shape,
            [vmem] * 3,
            vmem,
            [wide, pltpu.VMEM((degree_count + LANES, 4 * LANES), BF16)],
            24,
            800_000_000,
            received,
            lat_w,
            spread,
        )

    def filter_rows(contracted, received):
        return kernel_call(
            functools.partial(filter_kernel, contracted),
            degree_shape,
            [smem, smem, vmem, vmem, vmem],
            vmem,
            [degree_wide, degree_wide],
            24,
            300_000_000,
            own,
            deg_order,
            received,
            filter_weight,
            first,
        )

    spectrum = kernel_call(
        dft_kernel,
        spectrum_shape,
        [vmem, vmem],
        vmem,
        [wide, held_table, stages],
        24,
        2_400_000_000,
        grid,
        table_back,
    )
    cot_bands = {0: cot_send[0]}
    arrived, cot_send = beside(spectrum, both, cot_send, groups[0], cot_bands)
    coeffs = analysis(arrived, True)
    coeffs, cot_send = beside(coeffs, "polar", cot_send, groups[1], cot_bands)
    filtered = filter_rows(0, coeffs)
    filtered = exchange(filtered, "polar")
    cot_bands = [cot_bands[k] for k in range(across)]
    arrived = exchange(synthesis(filtered, False), both)
    grad_spec, output_bands = kernel_call(
        middle_kernel,
        (spectrum_shape, jax.ShapeDtypeStruct(bands_shape, BF16)),
        [smem, vmem, vmem] + [far] * (1 + across),
        (vmem, far),
        [
            wide,
            held_table,
            held_bands,
            held_bands,
            held_rows,
            stages,
            linears,
            sems,
            sems((across,)),
            sems((rows,)),
        ],
        WHOLE,
        4_800_000_000,
        own,
        arrived,
        table_back,
        grid,
        *cot_bands,
    )
    output_moved = {}
    arrived, output_bands = beside(grad_spec, both, output_bands, groups[0][:3], output_moved)
    grad_filtered = analysis(arrived, False)
    grad_filtered, output_bands = beside(
        grad_filtered, "polar", output_bands, groups[1], output_moved
    )
    grad_coeffs = filter_rows(1, grad_filtered)
    grad_coeffs, grad_filtered = lax.optimization_barrier((grad_coeffs, grad_filtered))
    weight_terms = kernel_call(
        weight_kernel,
        jax.ShapeDtypeStruct(filter_weight.shape, BF16),
        [smem, smem, vmem, vmem, vmem],
        vmem,
        [degree_wide, degree_wide],
        24,
        1000,
        own,
        deg_order,
        grad_filtered,
        coeffs,
        first,
    )
    grad_coeffs, output_bands = beside(
        grad_coeffs, "polar", output_bands, (5,), output_moved
    )
    output_moved[0] = piece(output_bands, 0)
    grad_weight = lax.psum_scatter(
        weight_terms, "azimuth", scatter_dimension=1, tiled=True
    ).astype(F32)
    arrived = exchange(synthesis(grad_coeffs, True), both)
    grad_bands = kernel_call(
        last_kernel,
        jax.ShapeDtypeStruct(bands_shape, BF16),
        [smem, vmem, vmem] + [far] * across,
        far,
        [wide, held_bands, held_rows, linears, sems((across,)), sems((rows,))],
        LAST,
        2_400_000_000,
        own,
        arrived,
        table_back,
        *cot_bands,
    )
    output_moved = [output_moved[k] for k in range(across)]
    grad_bands, output_moved = lax.optimization_barrier((grad_bands, output_moved))
    output = join_bands(output_moved)
    grad_field = (
        exchange(grad_bands, "azimuth")
        .transpose(1, 0, 2, 3)
        .reshape(lat_rows, lon_cols, channels)
    )
    return (output, grad_field, grad_weight)


def solution(mesh):
    placed = (
        P("polar", "azimuth", None),
        P("polar", "azimuth", None),
        P(("polar", "azimuth"), None, None),
        P(),
        P("polar", None, None),
        P(),
        P(),
    )
    return jax.shard_map(
        body,
        mesh=mesh,
        in_specs=placed,
        out_specs=(
            P("polar", "azimuth", None),
            P("polar", "azimuth", None),
            P("polar", "azimuth", None),
        ),
        check_vma=False,
    )
```

```python
import functools
import math

import jax
import jax.numpy as jnp
from jax import lax
from jax.experimental import pallas as pl
from jax.experimental.pallas import tpu as pltpu
from jax.sharding import PartitionSpec as P

BF16 = jnp.bfloat16
F32 = jnp.float32
LANES = 128
ROW_PAD = 192
MIB = 1024 * 1024
WHOLE = 56
LAST = 52
APART = 56
PIECES = 4
GELU_A = math.sqrt(2.0 / math.pi)
GELU_B = 0.044715


def exchange(payload, axes):
    return lax.all_to_all(payload, axes, split_axis=0, concat_axis=0, tiled=True)


def message_row(row, half, slot, part):
    return row * 8 + half * 4 + slot * 2 + part


def unpack_rows(received, wide, row, slot, part, peers):
    halves = [
        wide[pl.ds(message_row(row, half, slot, part), peers, stride=24), :] for half in range(2)
    ]
    return jnp.concatenate(halves, axis=1)


def doubling(zero_at, slot, peers):
    place = slot * peers + lax.broadcasted_iota(jnp.int32, (peers, LANES), 0)
    return jnp.where(place == zero_at, 1.0, 2.0)


def clear_pads(stage, across, lon):
    start = lon // 16 * 16
    for j in range(across):
        stage[j * ROW_PAD + start : (j + 1) * ROW_PAD, :] = jnp.zeros(
            (ROW_PAD - start, stage.shape[1]), BF16
        )


def dft_row(table, grid_rows, zero_at, wide, row, peers):
    total = jnp.dot(table[...], grid_rows[...], preferred_element_type=F32)
    for slot in range(2):
        for part in range(2):
            start = (slot * 2 + part) * peers
            for half in range(2):
                block = total[start : start + peers, half * LANES : (half + 1) * LANES]
                if zero_at is not None:
                    block = block * doubling(zero_at, slot, peers)
                wide[pl.ds(message_row(row, half, slot, part), peers, stride=24), :] = block


def dft_kernel(grid, table_back, out, wide, table, stages):
    across, rows, lon, _ = grid.shape
    peers = out.shape[0]
    table[...] = table_back[...].T
    for row in range(rows):
        stage = stages.at[row]
        clear_pads(stage, across, lon)
        for j in range(across):
            stage[j * ROW_PAD : j * ROW_PAD + lon, :] = grid[j, row]
        dft_row(table, stage, None, wide, row, peers)
    out[...] = wide[...].reshape(out.shape).astype(BF16)


def analysis_kernel(weighted, received, lat_w, folded_far, out, wide, columns, folded, arrival):
    size = folded.shape[0] // PIECES
    fetches = [
        pltpu.make_async_copy(
            folded_far.at[pl.ds(c * size, size)], folded.at[pl.ds(c * size, size)], arrival.at[c]
        )
        for c in range(PIECES)
    ]
    for fetch in fetches:
        fetch.start()
    peers = received.shape[0]
    wide[...] = received[...].astype(F32).reshape(wide.shape)
    rows = received.shape[1] // 8
    for slot in range(2):
        for row in range(rows):
            start = (slot * rows + row) * peers
            for part in range(2):
                for half in range(2):
                    block = wide[
                        pl.ds(message_row(row, half, slot, part), peers, stride=24), :
                    ]
                    if weighted:
                        block = block * lat_w[row * peers : (row + 1) * peers, :]
                    lane = (part * 2 + half) * LANES
                    columns[start : start + peers, lane : lane + LANES] = block.astype(BF16)
    for fetch in fetches:
        fetch.wait()
    total = jnp.dot(folded[...], columns[...], preferred_element_type=F32).astype(BF16)
    groups = out.shape[0]
    for quarter in range(4):
        lanes = slice(quarter * LANES, (quarter + 1) * LANES)
        out[:, quarter * 16 : (quarter + 1) * 16, :] = total[:512, lanes].reshape(groups, 16, LANES)
    extra = total[512:528, :].astype(F32)
    tail = jnp.concatenate(
        [extra[0:1, q * LANES : (q + 1) * LANES] for q in range(4)]
        + [jnp.zeros((4, LANES), F32)],
        axis=0,
    )
    out[:, 64:72, :] = jnp.broadcast_to(tail.astype(BF16)[None], (groups, 8, LANES))


def synthesis_kernel(weighted, received, lat_w, spread, out, wide, degrees):
    peers = out.shape[0]
    groups = received.shape[0]
    rows = out.shape[1] // 8
    for quarter in range(4):
        lanes = slice(quarter * LANES, (quarter + 1) * LANES)
        degrees[:512, lanes] = received[:, quarter * 16 : (quarter + 1) * 16, :].reshape(512, LANES)
    tail = jnp.sum(received[...].astype(F32)[:, 64:72, :], axis=0)
    extra = jnp.concatenate([tail[q : q + 1, :] for q in range(4)], axis=1)
    first = lax.broadcasted_iota(jnp.int32, (128, 512), 0) == 0
    degrees[512:640, :] = jnp.where(first, extra, 0.0).astype(BF16)
    for slot in range(2):
        for row in range(rows):
            total = jnp.dot(
                spread[slot, row * peers : (row + 1) * peers, :],
                degrees[...],
                preferred_element_type=F32,
            )
            for part in range(2):
                for half in range(2):
                    lane = (part * 2 + half) * LANES
                    block = total[:, lane : lane + LANES]
                    if weighted:
                        block = block * lat_w[row * peers : (row + 1) * peers, :]
                    wide[pl.ds(message_row(row, half, slot, part), peers, stride=24), :] = block
    out[...] = wide[...].reshape(out.shape).astype(BF16)


def degree_rows(wide, index, groups):
    parts = []
    for part in range(2):
        halves = [
            wide[pl.ds((part * 2 + half) * 16 + index, groups, stride=72), :] for half in range(2)
        ]
        parts.append(jnp.concatenate(halves, axis=1))
    return jnp.concatenate(parts, axis=0)


def extra_rows(wide, groups):
    parts = []
    for part in range(2):
        halves = [
            wide[pl.ds(64 + part * 2 + half, groups, stride=72), :] for half in range(2)
        ]
        parts.append(jnp.concatenate(halves, axis=1))
    return jnp.concatenate(parts, axis=0)


def store_rows(wide, start_of, values, groups):
    for part in range(2):
        for half in range(2):
            wide[pl.ds(start_of(part * 2 + half), groups, stride=72), :] = values[
                part * groups : (part + 1) * groups, half * LANES : (half + 1) * LANES
            ]


def pair_masks(lowest, degree):
    partner = 511 - degree
    return (
        lowest >= 0,
        degree >= lowest,
        partner >= lowest,
        511 - lowest == degree,
        511 - lowest == partner,
    )


def lowest_waves(own, first, shape):
    column = lax.broadcasted_iota(jnp.int32, first.shape, 1) == own[0]
    lowest = jnp.sum(jnp.where(column, first[...], 0), axis=1, keepdims=True)
    return jnp.broadcast_to(jnp.concatenate([lowest, lowest], axis=0), shape)


def filter_kernel(contracted, own, blocks, received, weight, first, out, wide, result):
    groups = received.shape[0]
    dims = (((1,), (contracted,)), ((), ()))
    wide[...] = received[...].astype(F32).reshape(wide.shape)
    result[...] = jnp.zeros_like(result)
    extra = extra_rows(wide, groups)
    lowest = lowest_waves(own, first, extra.shape)
    extra_sum = jnp.zeros_like(extra)
    for index in range(8):
        mirror = 15 - index
        degree = blocks[2 * own[1]] * 8 + index
        _, near, far, extra_near, extra_far = pair_masks(lowest, degree)
        one = degree_rows(wide, index, groups)
        two = degree_rows(wide, mirror, groups)
        stacked = jnp.concatenate([one, two, extra], axis=0).astype(BF16)
        by_one = lax.dot_general(stacked, weight[index], dims, preferred_element_type=F32)
        by_two = lax.dot_general(stacked, weight[mirror], dims, preferred_element_type=F32)
        side = 2 * groups
        store_rows(
            wide=result,
            start_of=lambda quarter: quarter * 16 + index,
            values=jnp.where(near, by_one[:side], by_two[:side]),
            groups=groups,
        )
        store_rows(
            wide=result,
            start_of=lambda quarter: quarter * 16 + mirror,
            values=jnp.where(far, by_two[side : 2 * side], by_one[side : 2 * side]),
            groups=groups,
        )
        extra_sum = (
            extra_sum
            + jnp.where(extra_near, by_one[2 * side :], 0.0)
            + jnp.where(extra_far, by_two[2 * side :], 0.0)
        )
    store_rows(result, lambda quarter: 64 + quarter, extra_sum, groups)
    out[...] = result[...].reshape(out.shape).astype(BF16)


def weight_kernel(own, blocks, received, coeffs, first, grad_w, wide, wide_coeffs):
    groups = received.shape[0]
    wide[...] = received[...].astype(F32).reshape(wide.shape)
    wide_coeffs[...] = coeffs[...].astype(F32).reshape(wide.shape)
    extra = extra_rows(wide, groups)
    kept_extra = extra_rows(wide_coeffs, groups)
    lowest = lowest_waves(own, first, extra.shape)
    summed = (((0,), (0,)), ((), ()))
    for index in range(8):
        mirror = 15 - index
        degree = blocks[2 * own[1]] * 8 + index
        _, near, far, extra_near, extra_far = pair_masks(lowest, degree)
        one = degree_rows(wide, index, groups)
        two = degree_rows(wide, mirror, groups)
        stacked = jnp.concatenate([one, two, extra], axis=0).astype(BF16)
        kept_one = degree_rows(wide_coeffs, index, groups)
        kept_two = degree_rows(wide_coeffs, mirror, groups)
        kept_near = jnp.concatenate(
            [
                jnp.where(near, kept_one, 0.0),
                jnp.where(far, 0.0, kept_two),
                jnp.where(extra_near, kept_extra, 0.0),
            ],
            axis=0,
        ).astype(BF16)
        kept_far = jnp.concatenate(
            [
                jnp.where(near, 0.0, kept_one),
                jnp.where(far, kept_two, 0.0),
                jnp.where(extra_far, kept_extra, 0.0),
            ],
            axis=0,
        ).astype(BF16)
        for place, kept in ((index, kept_near), (mirror, kept_far)):
            grad_w[place] = lax.dot_general(
                kept, stacked, summed, preferred_element_type=F32
            ).astype(BF16)


def idft_row(table_back, wide, zero_at, row, peers, linear):
    pieces = []
    for slot in range(2):
        for part in range(2):
            halves = []
            for half in range(2):
                block = wide[pl.ds(message_row(row, half, slot, part), peers, stride=24), :]
                if zero_at is not None:
                    block = block * doubling(zero_at, slot, peers)
                halves.append(block.astype(BF16))
            pieces.append(jnp.concatenate(halves, axis=1))
    spectrum = jnp.concatenate(pieces, axis=0)
    linear[...] = jnp.dot(table_back[...], spectrum, preferred_element_type=F32)


def middle_kernel(own, received, table_back, grid_far, *refs):
    across, rows, lon, _ = grid_far.shape
    cot_far, spectrum, out_far = refs[:across], refs[across], refs[across + 1]
    wide, table, grid, cotangent, output, stages, linears = refs[across + 2 : across + 9]
    grid_in, cot_in, leaving = refs[across + 9 :]
    others = [pltpu.make_async_copy(grid_far, grid, grid_in)] + [
        pltpu.make_async_copy(cot_far[k], cotangent.at[own[0] ^ k], cot_in.at[k])
        for k in range(across)
    ]
    for copy in others:
        copy.start()
    zero_at = own[2]
    peers = received.shape[0]
    wide[...] = received[...].astype(F32).reshape(wide.shape)
    for row in range(rows):
        clear_pads(stages.at[row], across, lon)
        idft_row(table_back, wide, zero_at, row, peers, linears.at[row])
    table[...] = table_back[...].T
    for copy in others:
        copy.wait()
    leave = [
        pltpu.make_async_copy(output.at[row], out_far.at[:, row], leaving.at[row])
        for row in range(rows)
    ]
    for row in range(rows):
        linear, stage = linears.at[row], stages.at[row]
        for j in range(across):
            place = slice(j * ROW_PAD, j * ROW_PAD + lon)
            value = linear[place, :].astype(BF16).astype(F32)
            square = value * value
            bend = jnp.tanh(value * (GELU_A + (GELU_A * GELU_B) * square))
            gate = 0.5 + 0.5 * bend
            output[row, j] = (grid[j, row].astype(F32) + value * gate).astype(BF16)
            steep = value * (2.0 * GELU_A + (6.0 * GELU_A * GELU_B) * square)
            slope = gate + steep * (gate - gate * gate)
            stage[place, :] = (cotangent[j, row].astype(F32) * slope).astype(BF16)
        leave[row].start()
        dft_row(table, stage, zero_at, wide, row, peers)
    spectrum[...] = wide[...].reshape(spectrum.shape).astype(BF16)
    for copy in leave:
        copy.wait()


def last_kernel(own, received, table_back, *refs):
    across = len(refs) - 7
    cot_far, out_far = refs[:across], refs[across]
    wide, cotangent, output, linears, cot_in, leaving = refs[across + 1 :]
    _, rows, lon, _ = out_far.shape
    others = [
        pltpu.make_async_copy(cot_far[k], cotangent.at[own[0] ^ k], cot_in.at[k])
        for k in range(across)
    ]
    for copy in others:
        copy.start()
    peers = received.shape[0]
    wide[...] = received[...].astype(F32).reshape(wide.shape)
    leave = [
        pltpu.make_async_copy(output.at[row], out_far.at[:, row], leaving.at[row])
        for row in range(rows)
    ]
    for row in range(rows):
        linear = linears.at[row]
        idft_row(table_back, wide, None, row, peers, linear)
        if row == 0:
            for copy in others:
                copy.wait()
        for j in range(across):
            value = linear[j * ROW_PAD : j * ROW_PAD + lon, :].astype(BF16).astype(F32)
            output[row, j] = (cotangent[j, row].astype(F32) + value).astype(BF16)
        leave[row].start()
    for copy in leave:
        copy.wait()


def split_kernel(grid, *refs):
    lon, lat, _ = grid.shape
    wide = refs[-1]
    wide[: lon * lat, :] = grid[...].astype(F32).reshape(lon * lat, LANES)
    across, rows = refs[0].shape[:2]
    for j in range(across):
        for row in range(rows):
            refs[0][j, row] = wide[pl.ds(row * across + j, lon, stride=lat), :].astype(BF16)


def split_far_kernel(own, grid, *refs):
    lon, lat, channels = grid.shape
    across = len(refs) - 3
    outs, (wide, bands, leaving) = refs[:across], refs[across:]
    rows = outs[0].shape[0]
    for lane in range(0, channels, LANES):
        lanes = slice(lane, lane + LANES)
        wide[: lon * lat, :] = grid[:, :, lanes].astype(F32).reshape(lon * lat, LANES)
        for k in range(across):
            for row in range(rows):
                start = row * across + (own[0] ^ k)
                bands[k, row, :, lanes] = wide[pl.ds(start, lon, stride=lat), :].astype(BF16)
    copies = [
        pltpu.make_async_copy(bands.at[k], outs[k], leaving.at[k]) for k in range(across)
    ]
    for copy in copies:
        copy.start()
    for copy in copies:
        copy.wait()


def join_kernel(own, *refs):
    bands, out, wide = refs[:-2], refs[-2], refs[-1]
    lon, lat, _ = out.shape
    across, rows = len(bands), bands[0].shape[0]
    for k in range(across):
        for row in range(rows):
            start = row * across + (own[0] ^ k)
            wide[pl.ds(start, lon, stride=lat), :] = bands[k][row].astype(F32)
    out[...] = wide[: lon * lat, :].reshape(out.shape).astype(BF16)


def degree_tables_kernel(own, blocks, waves, legendre, folded, spread, ordered, chosen):
    slots, lat_all, degree_count = legendre.shape
    count = degree_count // 16
    own_waves = [waves[own[3] * slots + slot] for slot in range(slots)]
    step = lax.broadcasted_iota(jnp.int32, (8, degree_count), 0)
    lane = lax.broadcasted_iota(jnp.int32, (8, degree_count), 1)
    chosen[...] = jnp.zeros_like(chosen)
    for pair in range(count):
        for slot in range(slots):
            pieces = []
            for block in (2 * pair, 2 * pair + 1):
                degree = blocks[block] * 8 + step
                if slot:
                    degree = jnp.where(
                        degree == own_waves[0], degree_count, degree_count - 1 - degree
                    )
                pieces.append(jnp.where(degree == lane, 1.0, 0.0))
            chosen[slot, pair * 16 : (pair + 1) * 16, :] = jnp.concatenate(pieces, axis=0).astype(
                BF16
            )
    sixteen = lax.broadcasted_iota(jnp.int32, (16, degree_count), 0)
    lanes = lax.broadcasted_iota(jnp.int32, (16, degree_count), 1)
    last = jnp.where(jnp.logical_and(sixteen == 0, lanes == own_waves[1]), 1.0, 0.0)
    chosen[1, degree_count : degree_count + 16, :] = last.astype(BF16)
    turned = (((1,), (1,)), ((), ()))
    for slot in range(slots):
        plane = legendre[slot].astype(F32).reshape(-1, lat_all // 256, 8, degree_count)
        for row in range(lat_all // 256):
            ordered[row * 256 : (row + 1) * 256, :] = (
                plane[:, row].reshape(256, degree_count).astype(BF16)
            )
        spread[slot] = lax.dot_general(
            ordered[...], chosen[slot], turned, preferred_element_type=F32
        ).astype(BF16)
        folded[:, slot * lat_all : (slot + 1) * lat_all] = lax.dot_general(
            chosen[slot, : folded.shape[0], :], ordered[...], turned, preferred_element_type=F32
        ).astype(BF16)


def tables(waves, lon_count, across):
    block = lon_count // across
    place = jnp.arange(ROW_PAD, dtype=jnp.int32)[:, None]
    angle = (2.0 * math.pi / lon_count) * (place * waves[None, :] % lon_count).astype(F32)
    size = jnp.where(place < block, 1.0 / math.sqrt(lon_count), 0.0)
    cosine, sine = jnp.cos(angle) * size, jnp.sin(angle) * size
    turn = jnp.arange(across, dtype=jnp.int32)[:, None] * waves[None, :] % across
    turn = (2.0 * math.pi / across) * turn.astype(F32)
    turn_cos, turn_sin = jnp.cos(turn)[:, None, :], jnp.sin(turn)[:, None, :]
    real = (cosine * turn_cos - sine * turn_sin).astype(BF16)
    imag = -(sine * turn_cos + cosine * turn_sin).astype(BF16)
    half = waves.shape[0] // 2
    back = jnp.concatenate(
        [real[..., :half], imag[..., :half], real[..., half:], imag[..., half:]], axis=-1
    )
    return back.reshape(across * ROW_PAD, 2 * waves.shape[0])


def body(field, cotangent, legendre, lat_weight, filter_weight, wave_order, deg_order):
    polar_count = lax.axis_size("polar")
    across = lax.axis_size("azimuth")
    peers = polar_count * across
    both = ("polar", "azimuth")
    lat_rows, lon_cols, channels = field.shape
    rows = lat_rows // across
    slots, lat_all, degree_count = legendre.shape
    block_size = degree_count // deg_order.shape[0]
    polar, azimuth = lax.axis_index("polar"), lax.axis_index("azimuth")
    device = polar * across + azimuth
    lon_count = lon_cols * across

    vmem = pl.BlockSpec(memory_space=pltpu.VMEM)
    smem = pl.BlockSpec(memory_space=pltpu.SMEM)
    far = pl.BlockSpec(memory_space=pltpu.HBM)
    pairs = wave_order.reshape(peers, slots)
    waves = pairs.T.reshape(-1)
    zero_at = jnp.sum(jnp.where(waves == 0, jnp.arange(waves.shape[0], dtype=jnp.int32), 0))
    own = jnp.stack([azimuth, polar, zero_at, device])
    band = (rows, lon_cols, channels)
    bands_shape = (across, *band)
    one_band = jax.ShapeDtypeStruct(band, BF16)
    trade = [[(i, i ^ k) for i in range(across)] for k in range(across)]

    def kernel_call(kernel, outs, in_specs, out_specs, scratch, mib, cost, *operands):
        return pl.pallas_call(
            kernel,
            out_shape=outs,
            in_specs=in_specs,
            out_specs=out_specs,
            scratch_shapes=scratch,
            compiler_params=pltpu.CompilerParams(vmem_limit_bytes=mib * MIB),
            cost_estimate=pl.CostEstimate(
                flops=cost, bytes_accessed=cost // 1000, transcendentals=0
            ),
        )(*operands)

    def half_bands(kernel, ins, outs, scalars, *operands):
        def spec(array):
            inner = tuple(array.shape[:-1])
            return pl.BlockSpec((*inner, LANES), lambda h: (0,) * len(inner) + (h,))

        return pl.pallas_call(
            kernel,
            grid=(channels // LANES,),
            out_shape=outs,
            in_specs=[smem] * len(scalars) + [spec(x) for x in ins],
            out_specs=jax.tree.map(spec, outs),
            scratch_shapes=[pltpu.VMEM(((ROW_PAD + 1) * lat_rows, LANES), F32)],
            compiler_params=pltpu.CompilerParams(vmem_limit_bytes=56 * MIB),
            cost_estimate=pl.CostEstimate(flops=2_000, bytes_accessed=2_000, transcendentals=0),
        )(*scalars, *operands)

    def join_bands(bands):
        out = jax.ShapeDtypeStruct((lon_cols, lat_rows, channels), BF16)
        return jnp.transpose(half_bands(join_kernel, bands, out, [own], *bands), (1, 0, 2))

    def piece(bands, k):
        if isinstance(bands, (list, tuple)):
            return bands[k]
        return lax.dynamic_index_in_dim(bands, azimuth ^ k, 0, keepdims=False)

    def beside(payload, axes, bands, kinds, done):
        payload, bands = lax.optimization_barrier((payload, bands))
        moved = [lax.ppermute(piece(bands, k), "azimuth", trade[k]) for k in kinds]
        payload = exchange(payload, axes)
        payload, bands, moved = lax.optimization_barrier((payload, bands, moved))
        done.update(zip(kinds, moved))
        return payload, bands

    groups = ((2, 6, 4, 5), (1, 3, 7))

    turned_field = jnp.transpose(field, (1, 0, 2))
    grid = exchange(
        half_bands(
            split_kernel,
            [turned_field],
            jax.ShapeDtypeStruct(bands_shape, BF16),
            [],
            turned_field,
        ),
        "azimuth",
    )

    table_back = tables(waves, lon_count, across)
    folded, spread = kernel_call(
        degree_tables_kernel,
        (
            jax.ShapeDtypeStruct((degree_count + LANES // 2, slots * lat_all), BF16),
            jax.ShapeDtypeStruct((slots, lat_all, degree_count + LANES), BF16),
        ),
        [smem, smem, smem, vmem],
        (vmem, vmem),
        [
            pltpu.VMEM((lat_all, degree_count), BF16),
            pltpu.VMEM((slots, degree_count + LANES, degree_count), BF16),
        ],
        32,
        1000,
        own,
        deg_order,
        wave_order,
        legendre,
    )
    lat_w = jnp.broadcast_to(
        lat_weight.reshape(polar_count, rows, across).transpose(1, 0, 2).reshape(-1, 1),
        (lat_all, LANES),
    )
    first = pairs[:, 0].reshape(polar_count, across)
    cot_send = kernel_call(
        split_far_kernel,
        (one_band,) * across,
        [smem, vmem],
        (far,) * across,
        [
            pltpu.VMEM(((ROW_PAD + 1) * lat_rows, LANES), F32),
            pltpu.VMEM(bands_shape, BF16),
            pltpu.SemaphoreType.DMA((across,)),
        ],
        24,
        1000,
        own,
        jnp.transpose(cotangent, (1, 0, 2)),
    )
    grid, table_back, folded, spread, lat_w, first, cot_send = lax.optimization_barrier(
        (grid, table_back, folded, spread, lat_w, first, cot_send)
    )

    message = (peers, 8 * rows, LANES)
    degree_message = (polar_count, 72, LANES)
    wide = pltpu.VMEM((peers * 8 * rows, LANES), F32)
    degree_wide = pltpu.VMEM((polar_count * 72, LANES), F32)
    stages = pltpu.VMEM((rows, across * ROW_PAD, channels), BF16)
    linears = pltpu.VMEM((rows, across * ROW_PAD, channels), F32)
    held_bands = pltpu.VMEM(bands_shape, BF16)
    held_rows = pltpu.VMEM((rows, across, lon_cols, channels), BF16)
    sems = pltpu.SemaphoreType.DMA
    held_table = pltpu.VMEM(table_back.shape[::-1], BF16)
    spectrum_shape = jax.ShapeDtypeStruct(message, BF16)
    degree_shape = jax.ShapeDtypeStruct(degree_message, BF16)
    local_degrees = filter_weight.shape[0]

    def analysis(received, weighted):
        return kernel_call(
            functools.partial(analysis_kernel, weighted),
            degree_shape,
            [vmem, vmem, far],
            vmem,
            [
                wide,
                pltpu.VMEM((slots * lat_all, 4 * LANES), BF16),
                pltpu.VMEM(folded.shape, BF16),
                sems((PIECES,)),
            ],
            APART,
            800_000_000,
            received,
            lat_w,
            folded,
        )

    def synthesis(received, weighted):
        return kernel_call(
            functools.partial(synthesis_kernel, weighted),
            spectrum_shape,
            [vmem] * 3,
            vmem,
            [wide, pltpu.VMEM((degree_count + LANES, 4 * LANES), BF16)],
            24,
            800_000_000,
            received,
            lat_w,
            spread,
        )

    def filter_rows(contracted, received):
        return kernel_call(
            functools.partial(filter_kernel, contracted),
            degree_shape,
            [smem, smem, vmem, vmem, vmem],
            vmem,
            [degree_wide, degree_wide],
            24,
            300_000_000,
            own,
            deg_order,
            received,
            filter_weight,
            first,
        )

    spectrum = kernel_call(
        dft_kernel,
        spectrum_shape,
        [vmem, vmem],
        vmem,
        [wide, held_table, stages],
        24,
        2_400_000_000,
        grid,
        table_back,
    )
    cot_bands = {0: cot_send[0]}
    arrived, cot_send = beside(spectrum, both, cot_send, groups[0], cot_bands)
    coeffs = analysis(arrived, True)
    coeffs, cot_send = beside(coeffs, "polar", cot_send, groups[1], cot_bands)
    filtered = filter_rows(0, coeffs)
    filtered = exchange(filtered, "polar")
    cot_bands = [cot_bands[k] for k in range(across)]
    arrived = exchange(synthesis(filtered, False), both)
    grad_spec, output_bands = kernel_call(
        middle_kernel,
        (spectrum_shape, jax.ShapeDtypeStruct(bands_shape, BF16)),
        [smem, vmem, vmem] + [far] * (1 + across),
        (vmem, far),
        [
            wide,
            held_table,
            held_bands,
            held_bands,
            held_rows,
            stages,
            linears,
            sems,
            sems((across,)),
            sems((rows,)),
        ],
        WHOLE,
        4_800_000_000,
        own,
        arrived,
        table_back,
        grid,
        *cot_bands,
    )
    output_moved = {}
    arrived, output_bands = beside(grad_spec, both, output_bands, groups[0][:3], output_moved)
    grad_filtered = analysis(arrived, False)
    grad_filtered, output_bands = beside(
        grad_filtered, "polar", output_bands, groups[1], output_moved
    )
    grad_coeffs = filter_rows(1, grad_filtered)
    grad_coeffs, grad_filtered = lax.optimization_barrier((grad_coeffs, grad_filtered))
    weight_terms = kernel_call(
        weight_kernel,
        jax.ShapeDtypeStruct(filter_weight.shape, BF16),
        [smem, smem, vmem, vmem, vmem],
        vmem,
        [degree_wide, degree_wide],
        24,
        1000,
        own,
        deg_order,
        grad_filtered,
        coeffs,
        first,
    )
    grad_coeffs, output_bands = beside(
        grad_coeffs, "polar", output_bands, (5,), output_moved
    )
    output_moved[0] = piece(output_bands, 0)
    grad_weight = lax.psum_scatter(
        weight_terms, "azimuth", scatter_dimension=1, tiled=True
    ).astype(F32)
    arrived = exchange(synthesis(grad_coeffs, True), both)
    grad_bands = kernel_call(
        last_kernel,
        jax.ShapeDtypeStruct(bands_shape, BF16),
        [smem, vmem, vmem] + [far] * across,
        far,
        [wide, held_bands, held_rows, linears, sems((across,)), sems((rows,))],
        LAST,
        2_400_000_000,
        own,
        arrived,
        table_back,
        *cot_bands,
    )
    output_moved = [output_moved[k] for k in range(across)]
    grad_bands, output_moved = lax.optimization_barrier((grad_bands, output_moved))
    output = join_bands(output_moved)
    grad_field = (
        exchange(grad_bands, "azimuth")
        .transpose(1, 0, 2, 3)
        .reshape(lat_rows, lon_cols, channels)
    )
    return (output, grad_field, grad_weight)


def solution(mesh):
    placed = (
        P("polar", "azimuth", None),
        P("polar", "azimuth", None),
        P(("polar", "azimuth"), None, None),
        P(),
        P("polar", None, None),
        P(),
        P(),
    )
    return jax.shard_map(
        body,
        mesh=mesh,
        in_specs=placed,
        out_specs=(
            P("polar", "azimuth", None),
            P("polar", "azimuth", None),
            P("polar", "azimuth", None),
        ),
        check_vma=False,
    )
```
